512 devices in a mesh: group: 8 (over z_lo, x), fsdp: 64 (over y, z_hi, core).
Axes of the slice: x: 4, y: 8, z: 8 (z_hi: 4, z_lo: 2; z = z_hi * 2 + z_lo), core: 2. Of those that a mesh axis runs over, the one named last changes fastest.
Arguments:
- hidden: bfloat16 [8, 11776, 8192], P('group', 'fsdp'), may hold values from -6 to 6
- cotangent: bfloat16 [8, 11776, 512], P('group', 'fsdp'), may hold values from -0.4375 to 0.4375
- weight: float32 [8, 8192, 512], P('group', 'fsdp'), may hold values from -6 to 6
- first_moment: bfloat16 [8, 8192, 512], P('group', 'fsdp'), may hold values from -12 to 12
- second_moment: bfloat16 [8, 8192, 512], P('group', 'fsdp'), may hold values from 1 to 100
- sync_frag: int32 [1], replicated, may hold values from 0 to 5
- frag_local: float32 [8, 8192, 512], P('group', 'fsdp'), may hold values from -6 to 6
- frag_anchor: float32 [6, 8192, 512], P(None, ('fsdp', 'group')), may hold values from -6 to 6
- frag_momentum: float32 [6, 8192, 512], P(None, ('fsdp', 'group')), may hold values from -3 to 3
Outputs:
- new_weight: float32 [8, 8192, 512], P('group', 'fsdp')
- new_first: bfloat16 [8, 8192, 512], P('group', 'fsdp')
- new_second: bfloat16 [8, 8192, 512], P('group', 'fsdp')
- new_local: float32 [8, 8192, 512], P('group', 'fsdp')
- new_anchor: float32 [8192, 512], P(('fsdp', 'group'))
- new_momentum: float32 [8192, 512], P(('fsdp', 'group'))
The draws below stay inside these ranges and needn't reach their ends.
All inputs are finite; a program needn't handle non-finite values.
Results may differ from the reference program's by a relative error of at most 0.0065.
Values may be sent and summed in bfloat16 or wider, within the bound.
A program may use at most 64 MiB of HBM per device.

```python
import math
import jax
import jax.numpy as jnp
from jax import lax

D = 8192
KW = 512
FRAGS = 6
TOK_DEV = 184
GTOK = 11776
GROUPS = 8


def levels(rng, extent, cuts, smallest, top_value):
    def one(axis_at, blocks):
        draws = jax.random.uniform(jax.random.fold_in(jax.random.fold_in(rng, 6), axis_at), (blocks,), jnp.float32, smallest / len(cuts), top_value / len(cuts))
        return jnp.repeat(jnp.exp(draws), extent[axis_at] // blocks).reshape((-1,) + (1,) * (len(extent) - axis_at - 1))

    factor_of = one(*cuts[0])
    for cut in cuts[1:]:
        factor_of = factor_of * one(*cut)
    return factor_of


def noise(stream_key, shape, spread, bound, shards=(), dtype=jnp.bfloat16):
    loudness = levels(stream_key, shape, shards, -0.22, 0.18) if shards else 1.0
    array = jax.random.normal(stream_key, shape, jnp.float32) * spread * loudness
    return jnp.minimum(jnp.maximum(array, -bound), bound).astype(dtype)


def setup_inputs(seed: int = 0) -> dict:
    keys = jax.random.split(jax.random.key(seed), 10)
    return {
        "hidden": noise(keys[0], (GROUPS, GTOK, D), 1.0, 6.0, ((0, 8), (1, 64))),
        "cotangent": noise(keys[1], (GROUPS, GTOK, KW), TOK_DEV ** -0.5, 0.4375, ((0, 8), (1, 64))),
        "weight": noise(keys[2], (GROUPS, D, KW), 1.0, 6.0, ((0, 8), (1, 64)), jnp.float32),
        "first_moment": noise(keys[3], (GROUPS, D, KW), 2.0, 12.0, ((0, 8), (1, 64))),
        "second_moment": jnp.clip(jnp.exp(math.log(100.0) - 4.6051702 * jax.random.uniform(keys[4], (GROUPS, D, KW), jnp.float32) ** levels(keys[4], (GROUPS, D, KW), ((0, 8), (1, 64)), -0.2, 0.2)), 1.0, 100.0).astype(jnp.bfloat16),
        "sync_frag": jax.random.randint(keys[5], (1,), 0, FRAGS).astype(jnp.int32),
        "frag_local": noise(keys[6], (GROUPS, D, KW), 1.0, 6.0, ((0, 8), (1, 64)), jnp.float32),
        "frag_anchor": noise(keys[7], (FRAGS, D, KW), 1.0, 6.0, ((1, 512),), jnp.float32),
        "frag_momentum": noise(keys[8], (FRAGS, D, KW), 0.5, 3.0, ((1, 512),), jnp.float32),
    }


beta_one = 0.9
beta_two = 0.95
bias_one = 1.0 - 0.9 ** 10
bias_two = 1.0 - 0.95 ** 10
inner_rate = 0.01
weight_decay = 0.1
epsilon = 1e-08
outer_rate = 0.7
outer_mu = 0.9
mixing = 0.5

def one_group(operands):
    features, cotans = operands
    return jnp.dot(features.T, cotans, preferred_element_type=jnp.float32)

def reference(hidden, cotangent, weight, first_moment, second_moment, sync_frag, frag_local, frag_anchor, frag_momentum):
    gradient = lax.map(one_group, (hidden, cotangent))
    moment_one = beta_one * first_moment.astype(jnp.float32) + (1.0 - beta_one) * gradient
    moment_two = beta_two * second_moment.astype(jnp.float32) + (1.0 - beta_two) * gradient * gradient
    step_size = moment_one / bias_one / (jnp.sqrt(moment_two / bias_two) + epsilon)
    new_weight = weight - inner_rate * (step_size + weight_decay * weight)
    chosen = sync_frag[0].astype(jnp.int32)
    local = frag_local
    anchor = lax.dynamic_index_in_dim(frag_anchor, chosen, 0, keepdims=False)
    momentum = lax.dynamic_index_in_dim(frag_momentum, chosen, 0, keepdims=False)
    mean_delta = lax.optimization_barrier(jnp.mean(anchor[None] - local, axis=0))
    new_momentum = outer_mu * momentum + mean_delta
    new_anchor = anchor - outer_rate * (mean_delta + outer_mu * new_momentum)
    new_local = mixing * local + (1.0 - mixing) * new_anchor[None]
    return (new_weight, moment_one.astype(jnp.bfloat16), moment_two.astype(jnp.bfloat16), new_local, new_anchor, new_momentum)
```

```python
import heapq

import jax
import jax.numpy as jnp
from jax import lax
from jax.experimental import pallas as pl
from jax.experimental.pallas import tpu as pltpu
from jax.sharding import PartitionSpec as P

beta_one = 0.9
beta_two = 0.95
bias_one = 1.0 - 0.9**10
bias_two = 1.0 - 0.95**10
inner_rate = 0.01
weight_decay = 0.1
epsilon = 1e-08
outer_rate = 0.7
outer_mu = 0.9
mixing = 0.5

NY, NZ, NC = 8, 4, 2
DYS = (4, 3, -3, 2, -2, 1, -1, 0)
DZS = (2, 1, -1, 0)
UP, DOWN = 0, 1
SIGN = (1, -1)
R1 = 336
H1 = 176
H2 = 96
LANES = 128


def key_order(first):
    order = [(4, dz) for dz in DZS[:first]]
    for dz in DZS:
        order += [(dy, dz) for dy in DYS if (dy, dz) not in order]
    return order


SLOTS = key_order(3)
SLOT = {block: i for i, block in enumerate(SLOTS)}


def schedule():
    link_latency, dot_cost, add_cost = 1.5, 0.16, 0.15
    rate = {"y": 0.050, "z": 0.025}
    size = lambda rows: rows * LANES * 2 / 1e6
    parts1 = (H1, R1 - H1)
    whole2 = 512 - R1
    parts2 = (H2, whole2 - H2)
    steps = {}
    rank = 0

    def add(name, needs, cost, sends, priority):
        steps[name] = (needs, cost, sends, priority)

    for i, block in enumerate(SLOTS):
        add(("dot",) + block, [], dot_cost, [], 3.0 + i * 0.3)
    for s, dz in enumerate(DZS):
        for h in range(NY // 2):
            for d in (UP, DOWN):
                needs = [("dot", 4 if h == 0 else SIGN[d] * (4 - h), dz)]
                if h:
                    needs.append(("y1", s, h - 1, d))
                rows = parts1[d] if h == 0 else R1
                add(("y1", s, h, d), needs, add_cost, [("y", d, size(rows))], s * 1.5 + h)
    both = lambda name, s, h: [(name, s, h, UP), (name, s, h, DOWN)]
    add(("z1", 0, 0), [("dot", 0, 2)] + both("y1", 0, 3), 2 * add_cost,
        [("z", UP, size(parts1[0])), ("z", DOWN, size(parts1[1]))], -2.0)
    for d in (UP, DOWN):
        s = 1 + d
        add(("z1", 1, d), [("dot", 0, DZS[s]), ("z1", 0, 0)] + both("y1", s, 3), 2 * add_cost,
            [("z", d, size(R1))], -2.0)
    add(("z1", 2), [("dot", 0, 0), ("z1", 1, UP), ("z1", 1, DOWN)] + both("y1", 3, 3), 2 * add_cost, [], -2.0)
    for k, dy in enumerate(DYS):
        for h in range(NZ // 2):
            for d in (UP, DOWN):
                needs = [("dot", dy, 2 if h == 0 else SIGN[d])]
                if h:
                    needs.append(("z2", k, 0, d))
                rows = parts2[d] if h == 0 else whole2
                add(("z2", k, h, d), needs, add_cost, [("z", d, size(rows))], k * 0.7 + h * 1.2)
    for h in range(NY // 2):
        for d in (UP, DOWN):
            k = 0 if h == 0 else 2 * h - 1 + d
            needs = [("dot", DYS[k], 0)] + both("z2", k, 1)
            if h:
                needs.append(("y2", h - 1, d))
            rows = parts2[d] if h == 0 else whole2
            add(("y2", h, d), needs, 1.5 * add_cost, [("y", d, size(rows))], -1.0)
    add(("y2", 4), [("dot", 0, 0), ("y2", 3, UP), ("y2", 3, DOWN)] + both("z2", 7, 1), 2 * add_cost, [], -1.0)

    done = {}
    free = {(a, d): 0.0 for a in "yz" for d in (UP, DOWN)}
    now, order = 0.0, []
    left = dict(steps)
    while left:
        best = None
        for name, (needs, cost, sends, priority) in left.items():
            if all(n in done for n in needs):
                ready = max([done[n] for n in needs], default=0.0)
                candidate = (max(ready, now), priority, name)
                if best is None or (candidate[0], candidate[1]) < (best[0], best[1]):
                    best = candidate
        start, _, name = best
        needs, cost, sends, _ = left.pop(name)
        now = start + cost
        done[name] = now
        for axis, d, amount in sends:
            begin = max(free[axis, d], now)
            free[axis, d] = begin + amount / rate[axis]
            done[name] = max(done[name], free[axis, d] + link_latency)
        order.append(name)
    return order, now, free


ORDER = schedule()[0]


def kernel(
    hid, cot, chosen, local, anchor, mom,
    grad_out, local_out, anchor_out, mom_out,
    h_own, h_peer, c_own, c_peer, ct, part, fin,
    y1a, y1b, y1w, z1a, z1b, z1w, z2a, z2b, z2w, y2a, y2b, y2w,
    l_own, l_in, a_all, m_all, a_send, a_in,
    load_sem, peer_send, peer_recv, send_sem, recv_sem, group_send, group_recv,
):
    group = lax.axis_index("group")
    me = lax.axis_index("fsdp")
    groups = lax.axis_size("group")
    y, z, core = me // (NZ * NC), (me // NC) % NZ, me % NC
    place = lambda yy, zz, cc: (lax.rem(yy + NY, NY) * NZ + lax.rem(zz + NZ, NZ)) * NC + cc
    peer = (group, place(y, z, 1 - core))
    partner = {
        "y": [(group, place(y + sign, z, core)) for sign in SIGN],
        "z": [(group, place(y, z + sign, core)) for sign in SIGN],
    }
    members = [(lax.rem(group + r, groups), me) for r in range(1, groups)]
    sublength = anchor.shape[1]

    loads = {}

    def load(name, source, target):
        loads[name] = pltpu.make_async_copy(source, target, load_sem.at[len(loads)])
        loads[name].start()

    def columns(block, cc):
        at = pl.multiple_of(place(y + block[0], z + block[1], cc) * LANES, LANES)
        return hid.at[0, :, pl.ds(at, LANES)]

    load("cot", cot.at[0], c_own)
    for i, block in enumerate(SLOTS):
        load(block, columns(block, core), h_own.at[i])
    load("local", local.at[0], l_own)
    load("anchor", anchor, a_all)
    load("mom", mom, m_all)

    barrier = pltpu.get_barrier_semaphore()
    everyone = [peer] + partner["y"] + partner["z"] + members
    for device in everyone:
        pl.semaphore_signal(barrier, inc=1, device_id=device, device_id_type=pl.DeviceIdType.MESH)
    pl.semaphore_wait(barrier, len(everyone))

    def remote(source, target, send, recv, device):
        return pltpu.make_async_remote_copy(
            src_ref=source, dst_ref=target, send_sem=send, recv_sem=recv,
            device_id=device, device_id_type=pl.DeviceIdType.MESH,
        )

    swaps = [remote(cot.at[0], c_peer, peer_send.at[0], peer_recv.at[0], peer)]
    swaps[0].start()
    for i, block in enumerate(SLOTS):
        swaps.append(
            remote(columns(block, 1 - core), h_peer.at[i], peer_send.at[1 + i], peer_recv.at[1 + i], peer)
        )
        swaps[-1].start()
    spread = []
    for r, device in enumerate(members):
        rows = pl.ds(pl.multiple_of(device[0] * sublength, sublength), sublength)
        spread.append(
            remote(local.at[0, rows], l_in.at[r], group_send.at[r], group_recv.at[r], device)
        )
        spread[-1].start()

    loads["cot"].wait()
    ct[0] = jnp.transpose(c_own[...].astype(jnp.float32)).astype(jnp.bfloat16)
    swaps[0].wait_recv()
    ct[1] = jnp.transpose(c_peer[...].astype(jnp.float32)).astype(jnp.bfloat16)

    messages = {}

    def send(name, axis, d, bufs, index, value):
        number = len(messages)
        out, into = bufs.at[(0,) + index], bufs.at[(1,) + index]
        out[...] = value.astype(jnp.bfloat16)
        messages[name] = (
            remote(out, into, send_sem.at[number], recv_sem.at[number], partner[axis][d]), into,
        )
        messages[name][0].start()

    def arrived(name):
        copy, into = messages[name]
        copy.wait_recv()
        return into[...].astype(jnp.float32)

    def own(dy, dz, begin, end):
        return part[SLOT[dy, dz], begin:end, :]

    def with_part(name, d, whole, cut):
        came = arrived(name)
        if d == UP:
            return jnp.concatenate([whole[:cut] + came, whole[cut:]], axis=0)
        return jnp.concatenate([whole[:cut], whole[cut:] + came], axis=0)

    def step_dot(dy, dz):
        i = SLOT[dy, dz]
        loads[dy, dz].wait()
        swaps[1 + i].wait_recv()
        part[i] = jnp.dot(ct[0], h_own[i], preferred_element_type=jnp.float32) + jnp.dot(
            ct[1], h_peer[i], preferred_element_type=jnp.float32
        )

    def step_y1(s, h, d):
        dz = DZS[s]
        if h == 0:
            begin, end = ((0, H1), (H1, R1))[d]
            send(("y1", s, h, d), "y", d, (y1a, y1b)[d], (s,), own(4, dz, begin, end))
            return
        whole = own(SIGN[d] * (4 - h), dz, 0, R1)
        if h == 1:
            whole = with_part(("y1", s, 0, d), d, whole, H1)
        else:
            whole = whole + arrived(("y1", s, h - 1, d))
        send(("y1", s, h, d), "y", d, y1w, (d, h - 1, s), whole)

    def y1_sum(s):
        return own(0, DZS[s], 0, R1) + arrived(("y1", s, 3, UP)) + arrived(("y1", s, 3, DOWN))

    def step_z1(h, d=None):
        if h == 0:
            whole = y1_sum(0)
            send(("z1", 0, UP), "z", UP, z1a, (), whole[:H1])
            send(("z1", 0, DOWN), "z", DOWN, z1b, (), whole[H1:])
        elif h == 1:
            whole = with_part(("z1", 0, d), d, y1_sum(1 + d), H1)
            send(("z1", 1, d), "z", d, z1w, (d,), whole)
        else:
            fin[0:R1, :] = y1_sum(3) + arrived(("z1", 1, UP)) + arrived(("z1", 1, DOWN))

    def step_z2(k, h, d):
        dy = DYS[k]
        if h == 0:
            begin, end = ((R1, R1 + H2), (R1 + H2, 512))[d]
            send(("z2", k, h, d), "z", d, (z2a, z2b)[d], (k,), own(dy, 2, begin, end))
            return
        whole = with_part(("z2", k, 0, d), d, own(dy, SIGN[d], R1, 512), H2)
        send(("z2", k, h, d), "z", d, z2w, (d, k), whole)

    def z2_sum(k):
        return own(DYS[k], 0, R1, 512) + arrived(("z2", k, 1, UP)) + arrived(("z2", k, 1, DOWN))

    far = []

    def step_y2(h, d=None):
        if h == 0:
            if not far:
                far.append(z2_sum(0))
            value = far[0][:H2] if d == UP else far[0][H2:]
            send(("y2", 0, d), "y", d, (y2a, y2b)[d], (), value)
        elif h < 4:
            whole = z2_sum(2 * h - 1 + d)
            if h == 1:
                whole = with_part(("y2", 0, d), d, whole, H2)
            else:
                whole = whole + arrived(("y2", h - 1, d))
            send(("y2", h, d), "y", d, y2w, (d, h - 1), whole)
        else:
            fin[R1:512, :] = z2_sum(7) + arrived(("y2", 3, UP)) + arrived(("y2", 3, DOWN))

    returned = []

    def outer_first():
        for name in ("local", "anchor", "mom"):
            loads[name].wait()
        at = pl.multiple_of(group * sublength, sublength)
        total = l_own[pl.ds(at, sublength), :]
        for r, copy in enumerate(spread):
            copy.wait_recv()
            total = total + l_in[r]
        f = chosen[0]
        here = a_all[f]
        mean_delta = here - total * (1.0 / groups)
        momentum_next = outer_mu * m_all[f] + mean_delta
        anchor_next = here - outer_rate * (mean_delta + outer_mu * momentum_next)
        anchor_out[...] = anchor_next
        mom_out[...] = momentum_next
        a_send[...] = anchor_next.astype(jnp.bfloat16)
        for r, device in enumerate(members):
            returned.append(
                remote(a_send, a_in.at[r], group_send.at[groups - 1 + r], group_recv.at[groups - 1 + r], device)
            )
            returned[-1].start()
        rows = pl.ds(at, sublength)
        local_out[rows, :] = mixing * l_own[rows, :] + (1.0 - mixing) * anchor_next

    def outer_second():
        for r, copy in enumerate(returned):
            copy.wait_recv()
            source = lax.rem(group + groups - 1 - r, groups)
            rows = pl.ds(pl.multiple_of(source * sublength, sublength), sublength)
            local_out[rows, :] = mixing * l_own[rows, :] + (1.0 - mixing) * a_in[r].astype(jnp.float32)

    run = {"dot": step_dot, "y1": step_y1, "z1": step_z1, "z2": step_z2, "y2": step_y2}
    for number, name in enumerate(ORDER):
        if number == len(ORDER) // 2:
            outer_first()
        if number == len(ORDER) * 3 // 4:
            outer_second()
        run[name[0]](*name[1:])

    grad_out[...] = jnp.transpose(fin[...])
    for copy in swaps + spread + returned + [copy for copy, _ in messages.values()]:
        copy.wait_send()


def reduced(hidden, cotangent, sync_frag, frag_local, frag_anchor, frag_momentum):
    tokens, keys = cotangent.shape[1:]
    frags, sublength, _ = frag_anchor.shape
    rows = frag_local.shape[1]
    groups = lax.axis_size("group")
    blocks = len(SLOTS)
    bf16, f32 = jnp.bfloat16, jnp.float32
    half1, half2 = (H1, R1 - H1), (H2, keys - R1 - H2)
    n1, n2 = R1, keys - R1
    messages = 2 * (16 + 2 + 16 + 4)
    vmem = pl.BlockSpec(memory_space=pltpu.VMEM)
    hbm = pl.BlockSpec(memory_space=pl.ANY)
    return pl.pallas_call(
        kernel,
        out_shape=(
            jax.ShapeDtypeStruct((rows, keys), f32),
            jax.ShapeDtypeStruct((rows, keys), f32),
            jax.ShapeDtypeStruct((sublength, keys), f32),
            jax.ShapeDtypeStruct((sublength, keys), f32),
        ),
        in_specs=[hbm, hbm, pl.BlockSpec(memory_space=pltpu.SMEM), hbm, hbm, hbm],
        out_specs=(vmem, vmem, vmem, vmem),
        scratch_shapes=[
            pltpu.VMEM((blocks, tokens, LANES), bf16),
            pltpu.VMEM((blocks, tokens, LANES), bf16),
            pltpu.VMEM((tokens, keys), bf16),
            pltpu.VMEM((tokens, keys), bf16),
            pltpu.VMEM((2, keys, tokens), bf16),
            pltpu.VMEM((blocks, keys, LANES), f32),
            pltpu.VMEM((keys, LANES), f32),
            pltpu.VMEM((2, NZ, half1[0], LANES), bf16),
            pltpu.VMEM((2, NZ, half1[1], LANES), bf16),
            pltpu.VMEM((2, 2, NY // 2 - 1, NZ, n1, LANES), bf16),
            pltpu.VMEM((2, half1[0], LANES), bf16),
            pltpu.VMEM((2, half1[1], LANES), bf16),
            pltpu.VMEM((2, 2, n1, LANES), bf16),
            pltpu.VMEM((2, NY, half2[0], LANES), bf16),
            pltpu.VMEM((2, NY, half2[1], LANES), bf16),
            pltpu.VMEM((2, 2, NY, n2, LANES), bf16),
            pltpu.VMEM((2, half2[0], LANES), bf16),
            pltpu.VMEM((2, half2[1], LANES), bf16),
            pltpu.VMEM((2, 2, NY // 2 - 1, n2, LANES), bf16),
            pltpu.VMEM((rows, keys), f32),
            pltpu.VMEM((groups - 1, sublength, keys), f32),
            pltpu.VMEM((frags, sublength, keys), f32),
            pltpu.VMEM((frags, sublength, keys), f32),
            pltpu.VMEM((sublength, keys), bf16),
            pltpu.VMEM((groups - 1, sublength, keys), bf16),
            pltpu.SemaphoreType.DMA((blocks + 4,)),
            pltpu.SemaphoreType.DMA((blocks + 1,)),
            pltpu.SemaphoreType.DMA((blocks + 1,)),
            pltpu.SemaphoreType.DMA((messages,)),
            pltpu.SemaphoreType.DMA((messages,)),
            pltpu.SemaphoreType.DMA((2 * (groups - 1),)),
            pltpu.SemaphoreType.DMA((2 * (groups - 1),)),
        ],
        compiler_params=pltpu.CompilerParams(
            collective_id=0, has_side_effects=True, vmem_limit_bytes=40 * 1024 * 1024
        ),
        name="reduce_and_sync",
    )(hidden, cotangent, sync_frag, frag_local, frag_anchor, frag_momentum)


def per_device(
    hidden,
    cotangent,
    weight,
    first_moment,
    second_moment,
    sync_frag,
    frag_local,
    frag_anchor,
    frag_momentum,
):
    gradient, new_local, anchor_out, momentum_out = reduced(
        hidden, cotangent, sync_frag, frag_local, frag_anchor, frag_momentum
    )
    moment_one = beta_one * first_moment[0].astype(jnp.float32) + (1.0 - beta_one) * gradient
    moment_two = (
        beta_two * second_moment[0].astype(jnp.float32) + (1.0 - beta_two) * gradient * gradient
    )
    step_size = moment_one / bias_one / (jnp.sqrt(moment_two / bias_two) + epsilon)
    master = weight[0]
    new_weight = master - inner_rate * (step_size + weight_decay * master)
    return (
        new_weight[None],
        moment_one.astype(jnp.bfloat16)[None],
        moment_two.astype(jnp.bfloat16)[None],
        new_local[None],
        anchor_out,
        momentum_out,
    )


def solution(mesh):
    in_specs = (
        P("group", "fsdp", None),
        P("group", "fsdp", None),
        P("group", "fsdp", None),
        P("group", "fsdp", None),
        P("group", "fsdp", None),
        P(),
        P("group", "fsdp", None),
        P(None, ("fsdp", "group"), None),
        P(None, ("fsdp", "group"), None),
    )
    out_specs = (
        P("group", "fsdp", None),
        P("group", "fsdp", None),
        P("group", "fsdp", None),
        P("group", "fsdp", None),
        P(("fsdp", "group"), None),
        P(("fsdp", "group"), None),
    )
    return jax.shard_map(
        per_device, mesh=mesh, in_specs=in_specs, out_specs=out_specs, check_vma=False
    )
```

```python
import jax
import jax.numpy as jnp
from jax import lax
from jax.experimental import pallas as pl
from jax.experimental.pallas import tpu as pltpu
from jax.sharding import PartitionSpec as P

beta_one = 0.9
beta_two = 0.95
bias_one = 1.0 - 0.9**10
bias_two = 1.0 - 0.95**10
inner_rate = 0.01
weight_decay = 0.1
epsilon = 1e-08
outer_rate = 0.7
outer_mu = 0.9
mixing = 0.5

NY, NZ, NC = 8, 4, 2
DYS = (4, 3, -3, 2, -2, 1, -1, 0)
DZS = (2, 1, -1, 0)
UP, DOWN = 0, 1
SIGN = (1, -1)
R1 = 352
H1 = 176
H2 = 80
LANES = 128


PAIRS = (
    (((4, 2), (4, 1)), ((4, -1), (4, 0)))
    + tuple(((dy, 2), (-dy, 2)) for dy in (3, 2, 1))
    + (((0, 2), (0, 0)),)
    + tuple(((dy, 1), (dy, -1)) for dy in (3, -3, 2, -2, 1, -1, 0))
    + tuple(((dy, 0), (-dy, 0)) for dy in (3, 2, 1))
)
SLOT = {block: (i, j) for i, pair in enumerate(PAIRS) for j, block in enumerate(pair)}

ORDER = (
    ("dot", 0), ("y1", 0, 0, 0), ("y1", 0, 0, 1), ("z2", 0, 0, 1), ("z2", 0, 0, 0), ("y1", 1, 0, 1),
    ("y1", 1, 0, 0), ("dot", 3), ("z2", 3, 0, 1), ("z2", 4, 0, 0), ("z2", 3, 0, 0), ("dot", 1),
    ("y1", 3, 0, 0), ("z2", 4, 0, 1), ("y1", 2, 0, 1), ("y1", 3, 0, 1), ("y1", 2, 0, 0), ("dot", 2),
    ("dot", 4), ("z2", 5, 0, 1), ("z2", 1, 0, 0), ("dot", 6), ("z2", 2, 0, 1), ("y1", 0, 1, 0),
    ("y1", 0, 1, 1), ("dot", 7), ("z2", 2, 0, 0), ("dot", 5), ("z2", 6, 0, 0), ("z2", 1, 0, 1),
    ("z2", 0, 1, 1), ("y1", 1, 1, 1), ("y1", 1, 1, 0), ("dot", 15), ("z2", 5, 0, 0), ("dot", 10),
    ("z2", 6, 0, 1), ("y1", 2, 1, 0), ("y1", 2, 1, 1), ("z2", 7, 0, 1), ("z2", 0, 1, 0), ("dot", 14),
    ("dot", 8), ("z2", 7, 0, 0), ("dot", 9), ("y1", 0, 2, 1), ("z2", 2, 1, 1), ("y1", 0, 2, 0),
    ("z2", 1, 1, 0), ("z2", 4, 1, 1), ("dot", 12), ("y1", 1, 2, 0), ("z2", 4, 1, 0), ("z2", 3, 1, 1),
    ("y1", 1, 2, 1), ("y1", 2, 2, 0), ("z2", 2, 1, 0), ("y1", 2, 2, 1), ("z2", 7, 1, 1), ("y1", 0, 3, 1),
    ("y1", 0, 3, 0), ("dot", 13), ("y2", 0, 1), ("y2", 0, 0), ("z2", 1, 1, 1), ("dot", 11), ("z2", 5, 1, 0),
    ("z2", 3, 1, 0), ("y1", 1, 3, 0), ("y1", 3, 1, 1), ("y1", 1, 3, 1), ("y1", 3, 1, 0), ("z1", 0, 0),
    ("y1", 2, 3, 1), ("y1", 2, 3, 0), ("z2", 5, 1, 1), ("z2", 6, 1, 1), ("z2", 7, 1, 0), ("y2", 1, 1),
    ("y2", 1, 0), ("y1", 3, 2, 1), ("z2", 6, 1, 0), ("y1", 3, 2, 0), ("z1", 1, 0), ("z1", 1, 1),
    ("y2", 2, 0), ("y2", 2, 1), ("y1", 3, 3, 0), ("y1", 3, 3, 1), ("y2", 3, 0), ("y2", 3, 1), ("z1", 2),
    ("y2", 4),
)

def kernel(
    hid, cot, chosen, local, anchor, mom,
    grad_out, local_out, anchor_out, mom_out,
    h_own, h_peer, c_own, c_peer, ct, part, fin,
    y1a, y1b, y1w, z1a, z1b, z1w, z2a, z2b, z2w, y2a, y2b, y2w,
    l_own, l_in, a_all, m_all, a_send, a_in,
    load_sem, peer_send, peer_recv, send_sem, recv_sem, group_send, group_recv,
):
    group = lax.axis_index("group")
    me = lax.axis_index("fsdp")
    groups = lax.axis_size("group")
    y, z, core = me // (NZ * NC), (me // NC) % NZ, me % NC
    place = lambda yy, zz, cc: (lax.rem(yy + NY, NY) * NZ + lax.rem(zz + NZ, NZ)) * NC + cc
    peer = (group, place(y, z, 1 - core))
    partner = {
        "y": [(group, place(y + sign, z, core)) for sign in SIGN],
        "z": [(group, place(y, z + sign, core)) for sign in SIGN],
    }
    members = [(lax.rem(group + r, groups), me) for r in range(1, groups)]
    sublength = anchor.shape[1]

    barrier = pltpu.get_barrier_semaphore()
    everyone = [peer] + partner["y"] + partner["z"] + members
    for device in everyone:
        pl.semaphore_signal(barrier, inc=1, device_id=device, device_id_type=pl.DeviceIdType.MESH)

    loads = {}

    def load(name, source, target):
        loads[name] = pltpu.make_async_copy(source, target, load_sem.at[len(loads)])
        loads[name].start()

    def columns(block, cc):
        at = pl.multiple_of(place(y + block[0], z + block[1], cc) * LANES, LANES)
        return hid.at[0, :, pl.ds(at, LANES)]

    def half(ref, block):
        i, j = SLOT[block]
        return ref.at[i, :, j * LANES : (j + 1) * LANES]

    load("cot", cot.at[0], c_own)
    for block in SLOT:
        load(block, columns(block, core), half(h_own, block))
    load("local", local.at[0], l_own)
    load("anchor", anchor, a_all)
    load("mom", mom, m_all)
    pl.semaphore_wait(barrier, len(everyone))

    def remote(source, target, send, recv, device):
        return pltpu.make_async_remote_copy(
            src_ref=source, dst_ref=target, send_sem=send, recv_sem=recv,
            device_id=device, device_id_type=pl.DeviceIdType.MESH,
        )

    swaps = {"cot": remote(cot.at[0], c_peer, peer_send.at[0], peer_recv.at[0], peer)}
    swaps["cot"].start()
    for i, block in enumerate(SLOT, 1):
        swaps[block] = remote(
            columns(block, 1 - core), half(h_peer, block), peer_send.at[i], peer_recv.at[i], peer
        )
        swaps[block].start()
    spread = []
    for r, device in enumerate(members):
        rows = pl.ds(pl.multiple_of(device[0] * sublength, sublength), sublength)
        spread.append(
            remote(local.at[0, rows], l_in.at[r], group_send.at[r], group_recv.at[r], device)
        )
        spread[-1].start()

    loads["cot"].wait()
    ct[0] = jnp.transpose(c_own[...].astype(jnp.float32)).astype(jnp.bfloat16)
    swaps["cot"].wait_recv()
    ct[1] = jnp.transpose(c_peer[...].astype(jnp.float32)).astype(jnp.bfloat16)

    messages = {}

    def send(name, axis, d, bufs, index, value):
        number = len(messages)
        out, into = bufs.at[(0,) + index], bufs.at[(1,) + index]
        out[...] = value.astype(jnp.bfloat16)
        messages[name] = (
            remote(out, into, send_sem.at[number], recv_sem.at[number], partner[axis][d]), into,
        )
        messages[name][0].start()

    def arrived(name):
        copy, into = messages[name]
        copy.wait_recv()
        return into[...].astype(jnp.float32)

    def own(dy, dz, begin, end):
        i, j = SLOT[dy, dz]
        return part[i, begin:end, j * LANES : (j + 1) * LANES]

    def with_part(name, d, whole, cut):
        came = arrived(name)
        if d == UP:
            return jnp.concatenate([whole[:cut] + came, whole[cut:]], axis=0)
        return jnp.concatenate([whole[:cut], whole[cut:] + came], axis=0)

    def step_dot(i):
        for block in PAIRS[i]:
            loads[block].wait()
            swaps[block].wait_recv()
        part[i] = jnp.dot(ct[0], h_own[i], preferred_element_type=jnp.float32) + jnp.dot(
            ct[1], h_peer[i], preferred_element_type=jnp.float32
        )

    def step_y1(s, h, d):
        dz = DZS[s]
        if h == 0:
            begin, end = ((0, H1), (H1, R1))[d]
            send(("y1", s, h, d), "y", d, (y1a, y1b)[d], (s,), own(4, dz, begin, end))
            return
        whole = own(SIGN[d] * (4 - h), dz, 0, R1)
        if h == 1:
            whole = with_part(("y1", s, 0, d), d, whole, H1)
        else:
            whole = whole + arrived(("y1", s, h - 1, d))
        send(("y1", s, h, d), "y", d, y1w, (d, h - 1, s), whole)

    def y1_sum(s):
        return own(0, DZS[s], 0, R1) + arrived(("y1", s, 3, UP)) + arrived(("y1", s, 3, DOWN))

    def step_z1(h, d=None):
        if h == 0:
            whole = y1_sum(0)
            send(("z1", 0, UP), "z", UP, z1a, (), whole[:H1])
            send(("z1", 0, DOWN), "z", DOWN, z1b, (), whole[H1:])
        elif h == 1:
            whole = with_part(("z1", 0, d), d, y1_sum(1 + d), H1)
            send(("z1", 1, d), "z", d, z1w, (d,), whole)
        else:
            fin[0:R1, :] = y1_sum(3) + arrived(("z1", 1, UP)) + arrived(("z1", 1, DOWN))

    def step_z2(k, h, d):
        dy = DYS[k]
        if h == 0:
            begin, end = ((R1, R1 + H2), (R1 + H2, 512))[d]
            send(("z2", k, h, d), "z", d, (z2a, z2b)[d], (k,), own(dy, 2, begin, end))
            return
        whole = with_part(("z2", k, 0, d), d, own(dy, SIGN[d], R1, 512), H2)
        send(("z2", k, h, d), "z", d, z2w, (d, k), whole)

    def z2_sum(k):
        return own(DYS[k], 0, R1, 512) + arrived(("z2", k, 1, UP)) + arrived(("z2", k, 1, DOWN))

    far = []

    def step_y2(h, d=None):
        if h == 0:
            if not far:
                far.append(z2_sum(0))
            value = far[0][:H2] if d == UP else far[0][H2:]
            send(("y2", 0, d), "y", d, (y2a, y2b)[d], (), value)
        elif h < 4:
            whole = z2_sum(2 * h - 1 + d)
            if h == 1:
                whole = with_part(("y2", 0, d), d, whole, H2)
            else:
                whole = whole + arrived(("y2", h - 1, d))
            send(("y2", h, d), "y", d, y2w, (d, h - 1), whole)
        else:
            fin[R1:512, :] = z2_sum(7) + arrived(("y2", 3, UP)) + arrived(("y2", 3, DOWN))

    returned = []

    def outer_first():
        for name in ("local", "anchor", "mom"):
            loads[name].wait()
        at = pl.multiple_of(group * sublength, sublength)
        total = l_own[pl.ds(at, sublength), :]
        for r, copy in enumerate(spread):
            copy.wait_recv()
            total = total + l_in[r]
        f = chosen[0]
        here = a_all[f]
        mean_delta = here - total * (1.0 / groups)
        momentum_next = outer_mu * m_all[f] + mean_delta
        anchor_next = here - outer_rate * (mean_delta + outer_mu * momentum_next)
        anchor_out[...] = anchor_next
        mom_out[...] = momentum_next
        a_send[...] = anchor_next.astype(jnp.bfloat16)
        for r, device in enumerate(members):
            returned.append(
                remote(a_send, a_in.at[r], group_send.at[groups - 1 + r], group_recv.at[groups - 1 + r], device)
            )
            returned[-1].start()
        rows = pl.ds(at, sublength)
        local_out[rows, :] = mixing * l_own[rows, :] + (1.0 - mixing) * anchor_next

    def outer_second():
        for r, copy in enumerate(returned):
            copy.wait_recv()
            source = lax.rem(group + groups - 1 - r, groups)
            rows = pl.ds(pl.multiple_of(source * sublength, sublength), sublength)
            local_out[rows, :] = mixing * l_own[rows, :] + (1.0 - mixing) * a_in[r].astype(jnp.float32)

    run = {"dot": step_dot, "y1": step_y1, "z1": step_z1, "z2": step_z2, "y2": step_y2}
    for number, name in enumerate(ORDER):
        if number == len(ORDER) // 2:
            outer_first()
        if number == len(ORDER) * 3 // 4:
            outer_second()
        run[name[0]](*name[1:])

    grad_out[...] = jnp.transpose(fin[...])
    for copy in list(swaps.values()) + spread + returned + [copy for copy, _ in messages.values()]:
        copy.wait_send()


def reduced(hidden, cotangent, sync_frag, frag_local, frag_anchor, frag_momentum):
    tokens, keys = cotangent.shape[1:]
    frags, sublength, _ = frag_anchor.shape
    rows = frag_local.shape[1]
    groups = lax.axis_size("group")
    pairs, blocks = len(PAIRS), len(SLOT)
    bf16, f32 = jnp.bfloat16, jnp.float32
    half1, half2 = (H1, R1 - H1), (H2, keys - R1 - H2)
    n1, n2 = R1, keys - R1
    messages = 2 * (16 + 2 + 16 + 4)
    vmem = pl.BlockSpec(memory_space=pltpu.VMEM)
    hbm = pl.BlockSpec(memory_space=pltpu.HBM)
    stay = lambda x: pltpu.with_memory_space_constraint(x, pltpu.HBM)
    return pl.pallas_call(
        kernel,
        out_shape=(
            jax.ShapeDtypeStruct((rows, keys), f32),
            jax.ShapeDtypeStruct((rows, keys), f32),
            jax.ShapeDtypeStruct((sublength, keys), f32),
            jax.ShapeDtypeStruct((sublength, keys), f32),
        ),
        in_specs=[hbm, hbm, pl.BlockSpec(memory_space=pltpu.SMEM), hbm, hbm, hbm],
        out_specs=(vmem, vmem, vmem, vmem),
        scratch_shapes=[
            pltpu.VMEM((pairs, tokens, 2 * LANES), bf16),
            pltpu.VMEM((pairs, tokens, 2 * LANES), bf16),
            pltpu.VMEM((tokens, keys), bf16),
            pltpu.VMEM((tokens, keys), bf16),
            pltpu.VMEM((2, keys, tokens), bf16),
            pltpu.VMEM((pairs, keys, 2 * LANES), f32),
            pltpu.VMEM((keys, LANES), f32),
            pltpu.VMEM((2, NZ, half1[0], LANES), bf16),
            pltpu.VMEM((2, NZ, half1[1], LANES), bf16),
            pltpu.VMEM((2, 2, NY // 2 - 1, NZ, n1, LANES), bf16),
            pltpu.VMEM((2, half1[0], LANES), bf16),
            pltpu.VMEM((2, half1[1], LANES), bf16),
            pltpu.VMEM((2, 2, n1, LANES), bf16),
            pltpu.VMEM((2, NY, half2[0], LANES), bf16),
            pltpu.VMEM((2, NY, half2[1], LANES), bf16),
            pltpu.VMEM((2, 2, NY, n2, LANES), bf16),
            pltpu.VMEM((2, half2[0], LANES), bf16),
            pltpu.VMEM((2, half2[1], LANES), bf16),
            pltpu.VMEM((2, 2, NY // 2 - 1, n2, LANES), bf16),
            pltpu.VMEM((rows, keys), f32),
            pltpu.VMEM((groups - 1, sublength, keys), f32),
            pltpu.VMEM((frags, sublength, keys), f32),
            pltpu.VMEM((frags, sublength, keys), f32),
            pltpu.VMEM((sublength, keys), bf16),
            pltpu.VMEM((groups - 1, sublength, keys), bf16),
            pltpu.SemaphoreType.DMA((blocks + 4,)),
            pltpu.SemaphoreType.DMA((blocks + 1,)),
            pltpu.SemaphoreType.DMA((blocks + 1,)),
            pltpu.SemaphoreType.DMA((messages,)),
            pltpu.SemaphoreType.DMA((messages,)),
            pltpu.SemaphoreType.DMA((2 * (groups - 1),)),
            pltpu.SemaphoreType.DMA((2 * (groups - 1),)),
        ],
        compiler_params=pltpu.CompilerParams(
            collective_id=0, has_side_effects=True, vmem_limit_bytes=40 * 1024 * 1024
        ),
        name="reduce_and_sync",
    )(stay(hidden), stay(cotangent), sync_frag, stay(frag_local), stay(frag_anchor), stay(frag_momentum))


def finish(
    gradient, weight, first, second, local, anchor, momentum,
    weight_out, first_out, second_out, local_out, anchor_out, momentum_out,
):
    slope = gradient[...]
    moment_one = beta_one * first[0].astype(jnp.float32) + (1.0 - beta_one) * slope
    moment_two = beta_two * second[0].astype(jnp.float32) + (1.0 - beta_two) * slope * slope
    step_size = moment_one / bias_one / (jnp.sqrt(moment_two / bias_two) + epsilon)
    master = weight[0]
    weight_out[0] = master - inner_rate * (step_size + weight_decay * master)
    first_out[0] = moment_one.astype(jnp.bfloat16)
    second_out[0] = moment_two.astype(jnp.bfloat16)
    local_out[0] = local[...]
    anchor_out[...] = anchor[...]
    momentum_out[...] = momentum[...]


def finished(gradient, weight, first, second, local, anchor, momentum):
    vmem = pl.BlockSpec(memory_space=pltpu.VMEM)
    shape = jax.ShapeDtypeStruct
    return pl.pallas_call(
        finish,
        out_shape=(
            shape(weight.shape, weight.dtype),
            shape(first.shape, first.dtype),
            shape(second.shape, second.dtype),
            shape(weight.shape, local.dtype),
            shape(anchor.shape, anchor.dtype),
            shape(momentum.shape, momentum.dtype),
        ),
        in_specs=[vmem] * 7,
        out_specs=(vmem,) * 6,
        compiler_params=pltpu.CompilerParams(vmem_limit_bytes=16 * 1024 * 1024),
        name="finish",
    )(gradient, weight, first, second, local, anchor, momentum)


def per_device(
    hidden,
    cotangent,
    weight,
    first_moment,
    second_moment,
    sync_frag,
    frag_local,
    frag_anchor,
    frag_momentum,
):
    gradient, new_local, anchor_out, momentum_out = reduced(
        hidden, cotangent, sync_frag, frag_local, frag_anchor, frag_momentum
    )
    return finished(
        gradient, weight, first_moment, second_moment, new_local, anchor_out, momentum_out
    )


def solution(mesh):
    in_specs = (
        P("group", "fsdp", None),
        P("group", "fsdp", None),
        P("group", "fsdp", None),
        P("group", "fsdp", None),
        P("group", "fsdp", None),
        P(),
        P("group", "fsdp", None),
        P(None, ("fsdp", "group"), None),
        P(None, ("fsdp", "group"), None),
    )
    out_specs = (
        P("group", "fsdp", None),
        P("group", "fsdp", None),
        P("group", "fsdp", None),
        P("group", "fsdp", None),
        P(("fsdp", "group"), None),
        P(("fsdp", "group"), None),
    )
    return jax.shard_map(
        per_device, mesh=mesh, in_specs=in_specs, out_specs=out_specs, check_vma=False
    )
```

```python
import jax
import jax.numpy as jnp
from jax import lax
from jax.experimental import pallas as pl
from jax.experimental.pallas import tpu as pltpu
from jax.sharding import PartitionSpec as P

beta_one = 0.9
beta_two = 0.95
bias_one = 1.0 - 0.9**10
bias_two = 1.0 - 0.95**10
inner_rate = 0.01
weight_decay = 0.1
epsilon = 1e-08
outer_rate = 0.7
outer_mu = 0.9
mixing = 0.5

NY, NZ, NC = 8, 4, 2
DYS = (4, 3, -3, 2, -2, 1, -1, 0)
DZS = (2, 1, -1, 0)
UP, DOWN = 0, 1
SIGN = (1, -1)
R1 = 352
H1 = 176
H2 = 80
LANES = 128


PAIRS = (
    (((4, 2), (4, 1)), ((4, -1), (4, 0)))
    + tuple(((dy, 2), (-dy, 2)) for dy in (3, 2, 1))
    + (((0, 2), (0, 0)),)
    + tuple(((dy, 1), (dy, -1)) for dy in (3, -3, 2, -2, 1, -1, 0))
    + tuple(((dy, 0), (-dy, 0)) for dy in (3, 2, 1))
)
SLOT = {block: (i, j) for i, pair in enumerate(PAIRS) for j, block in enumerate(pair)}

ORDER = (
    ("dot", 0), ("y1", 0, 0, 1), ("y1", 0, 0, 0), ("dot", 1), ("z2", 0, 0, 1), ("z2", 0, 0, 0),
    ("y1", 2, 0, 1), ("y1", 1, 0, 1), ("y1", 2, 0, 0), ("dot", 2), ("z2", 2, 0, 1), ("z2", 2, 0, 0),
    ("y1", 3, 0, 1), ("y1", 3, 0, 0), ("dot", 5), ("dot", 3), ("z2", 4, 0, 0), ("z2", 1, 0, 1),
    ("y1", 1, 0, 0), ("z2", 3, 0, 0), ("z2", 7, 0, 1), ("dot", 7), ("y1", 0, 1, 1), ("y1", 0, 1, 0),
    ("dot", 4), ("z2", 6, 0, 1), ("z2", 6, 0, 0), ("dot", 13), ("dot", 6), ("y1", 2, 1, 0), ("z2", 1, 0, 0),
    ("y1", 2, 1, 1), ("z2", 4, 0, 1), ("z2", 3, 0, 1), ("y1", 1, 1, 1), ("dot", 12), ("z2", 0, 1, 1),
    ("z2", 7, 0, 0), ("y1", 1, 1, 0), ("dot", 8), ("dot", 10), ("z2", 5, 0, 0), ("dot", 15), ("dot", 9),
    ("z2", 0, 1, 0), ("dot", 11), ("y1", 0, 2, 1), ("y1", 0, 2, 0), ("z2", 3, 1, 0), ("z2", 7, 1, 1),
    ("y1", 2, 2, 1), ("z2", 5, 0, 1), ("z2", 2, 1, 0), ("z2", 4, 1, 0), ("y1", 2, 2, 0), ("z2", 4, 1, 1),
    ("z2", 2, 1, 1), ("z2", 1, 1, 0), ("y1", 1, 2, 0), ("y1", 1, 2, 1), ("z2", 7, 1, 0), ("y1", 0, 3, 1),
    ("y1", 0, 3, 0), ("dot", 14), ("z2", 1, 1, 1), ("y1", 2, 3, 1), ("y2", 0, 0), ("y2", 0, 1),
    ("y1", 3, 1, 1), ("y1", 3, 1, 0), ("z2", 3, 1, 1), ("y1", 1, 3, 1), ("y1", 2, 3, 0), ("z1", 0, 0),
    ("y1", 1, 3, 0), ("z2", 5, 1, 0), ("y2", 1, 0), ("z2", 5, 1, 1), ("y2", 1, 1), ("y1", 3, 2, 1),
    ("y1", 3, 2, 0), ("z2", 6, 1, 1), ("z2", 6, 1, 0), ("z1", 1, 0), ("z1", 1, 1), ("y2", 2, 0),
    ("y2", 2, 1), ("y1", 3, 3, 1), ("y1", 3, 3, 0), ("y2", 3, 0), ("y2", 3, 1), ("z1", 2), ("y2", 4),
)


def kernel(
    hid, cot, chosen, local, anchor, mom,
    grad_out, local_out, anchor_out, mom_out,
    h_own, h_peer, c_own, c_peer, ct, part, fin,
    y1a, y1b, y1w, z1a, z1b, z1w, z2a, z2b, z2w, y2a, y2b, y2w,
    l_own, l_in, a_all, m_all, a_send, a_in,
    load_sem, peer_send, peer_recv, send_sem, recv_sem, group_send, group_recv,
):
    group = lax.axis_index("group")
    me = lax.axis_index("fsdp")
    groups = lax.axis_size("group")
    y, z, core = me // (NZ * NC), (me // NC) % NZ, me % NC
    place = lambda yy, zz, cc: (lax.rem(yy + NY, NY) * NZ + lax.rem(zz + NZ, NZ)) * NC + cc
    peer = (group, place(y, z, 1 - core))
    partner = {
        "y": [(group, place(y + sign, z, core)) for sign in SIGN],
        "z": [(group, place(y, z + sign, core)) for sign in SIGN],
    }
    members = [(lax.rem(group + r, groups), me) for r in range(1, groups)]
    sublength = anchor.shape[1]

    barrier = pltpu.get_barrier_semaphore()
    everyone = [peer] + partner["y"] + partner["z"] + members
    for device in everyone:
        pl.semaphore_signal(barrier, inc=1, device_id=device, device_id_type=pl.DeviceIdType.MESH)

    loads = {}

    def load(name, source, target):
        loads[name] = pltpu.make_async_copy(source, target, load_sem.at[len(loads)])
        loads[name].start()

    def columns(block, cc):
        at = pl.multiple_of(place(y + block[0], z + block[1], cc) * LANES, LANES)
        return hid.at[0, :, pl.ds(at, LANES)]

    def half(ref, block):
        i, j = SLOT[block]
        return ref.at[i, :, j * LANES : (j + 1) * LANES]

    def remote(source, target, send, recv, device):
        return pltpu.make_async_remote_copy(
            src_ref=source, dst_ref=target, send_sem=send, recv_sem=recv,
            device_id=device, device_id_type=pl.DeviceIdType.MESH,
        )

    swaps = {}

    def swap(name, source, target):
        number = len(swaps)
        swaps[name] = remote(source, target, peer_send.at[number], peer_recv.at[number], peer)
        swaps[name].start()

    def swap_blocks(blocks):
        for block in blocks:
            swap(block, columns(block, 1 - core), half(h_peer, block))

    def load_blocks(blocks):
        for block in blocks:
            load(block, columns(block, core), half(h_own, block))

    blocks = list(SLOT)
    load("cot", cot.at[0], c_own)
    pl.semaphore_wait(barrier, len(everyone))
    swap("cot", cot.at[0], c_peer)
    swap_blocks(blocks)
    load_blocks(blocks)
    load("local", local.at[0], l_own)
    load("anchor", anchor, a_all)
    load("mom", mom, m_all)
    spread = []
    for r, device in enumerate(members):
        rows = pl.ds(pl.multiple_of(device[0] * sublength, sublength), sublength)
        spread.append(
            remote(local.at[0, rows], l_in.at[r], group_send.at[r], group_recv.at[r], device)
        )
        spread[-1].start()
    loads["cot"].wait()
    ct[0] = jnp.transpose(c_own[...].astype(jnp.float32)).astype(jnp.bfloat16)
    swaps["cot"].wait_recv()
    ct[1] = jnp.transpose(c_peer[...].astype(jnp.float32)).astype(jnp.bfloat16)

    messages = {}

    def send(name, axis, d, bufs, index, value):
        number = len(messages)
        out, into = bufs.at[(0,) + index], bufs.at[(1,) + index]
        out[...] = value.astype(jnp.bfloat16)
        messages[name] = (
            remote(out, into, send_sem.at[number], recv_sem.at[number], partner[axis][d]), into,
        )
        messages[name][0].start()

    def arrived(name):
        copy, into = messages[name]
        copy.wait_recv()
        return into[...].astype(jnp.float32)

    def own(dy, dz, begin, end):
        i, j = SLOT[dy, dz]
        return part[i, begin:end, j * LANES : (j + 1) * LANES]

    def with_part(name, d, whole, cut):
        came = arrived(name)
        if d == UP:
            return jnp.concatenate([whole[:cut] + came, whole[cut:]], axis=0)
        return jnp.concatenate([whole[:cut], whole[cut:] + came], axis=0)

    def step_dot(i):
        for block in PAIRS[i]:
            loads[block].wait()
            swaps[block].wait_recv()
        part[i] = jnp.dot(ct[0], h_own[i], preferred_element_type=jnp.float32) + jnp.dot(
            ct[1], h_peer[i], preferred_element_type=jnp.float32
        )

    def step_y1(s, h, d):
        dz = DZS[s]
        if h == 0:
            begin, end = ((0, H1), (H1, R1))[d]
            send(("y1", s, h, d), "y", d, (y1a, y1b)[d], (s,), own(4, dz, begin, end))
            return
        whole = own(SIGN[d] * (4 - h), dz, 0, R1)
        if h == 1:
            whole = with_part(("y1", s, 0, d), d, whole, H1)
        else:
            whole = whole + arrived(("y1", s, h - 1, d))
        send(("y1", s, h, d), "y", d, y1w, (d, h - 1, s), whole)

    def y1_sum(s):
        return own(0, DZS[s], 0, R1) + arrived(("y1", s, 3, UP)) + arrived(("y1", s, 3, DOWN))

    def step_z1(h, d=None):
        if h == 0:
            whole = y1_sum(0)
            send(("z1", 0, UP), "z", UP, z1a, (), whole[:H1])
            send(("z1", 0, DOWN), "z", DOWN, z1b, (), whole[H1:])
        elif h == 1:
            whole = with_part(("z1", 0, d), d, y1_sum(1 + d), H1)
            send(("z1", 1, d), "z", d, z1w, (d,), whole)
        else:
            fin[0:R1, :] = y1_sum(3) + arrived(("z1", 1, UP)) + arrived(("z1", 1, DOWN))

    def step_z2(k, h, d):
        dy = DYS[k]
        if h == 0:
            begin, end = ((R1, R1 + H2), (R1 + H2, 512))[d]
            send(("z2", k, h, d), "z", d, (z2a, z2b)[d], (k,), own(dy, 2, begin, end))
            return
        whole = with_part(("z2", k, 0, d), d, own(dy, SIGN[d], R1, 512), H2)
        send(("z2", k, h, d), "z", d, z2w, (d, k), whole)

    def z2_sum(k):
        return own(DYS[k], 0, R1, 512) + arrived(("z2", k, 1, UP)) + arrived(("z2", k, 1, DOWN))

    far = []

    def step_y2(h, d=None):
        if h == 0:
            if not far:
                far.append(z2_sum(0))
            value = far[0][:H2] if d == UP else far[0][H2:]
            send(("y2", 0, d), "y", d, (y2a, y2b)[d], (), value)
        elif h < 4:
            whole = z2_sum(2 * h - 1 + d)
            if h == 1:
                whole = with_part(("y2", 0, d), d, whole, H2)
            else:
                whole = whole + arrived(("y2", h - 1, d))
            send(("y2", h, d), "y", d, y2w, (d, h - 1), whole)
        else:
            fin[R1:512, :] = z2_sum(7) + arrived(("y2", 3, UP)) + arrived(("y2", 3, DOWN))

    returned = []

    def outer_first():
        for name in ("local", "anchor", "mom"):
            loads[name].wait()
        at = pl.multiple_of(group * sublength, sublength)
        total = l_own[pl.ds(at, sublength), :]
        for r, copy in enumerate(spread):
            copy.wait_recv()
            total = total + l_in[r]
        f = chosen[0]
        here = a_all[f]
        mean_delta = here - total * (1.0 / groups)
        momentum_next = outer_mu * m_all[f] + mean_delta
        anchor_next = here - outer_rate * (mean_delta + outer_mu * momentum_next)
        anchor_out[...] = anchor_next
        mom_out[...] = momentum_next
        a_send[...] = anchor_next.astype(jnp.bfloat16)
        for r, device in enumerate(members):
            returned.append(
                remote(a_send, a_in.at[r], group_send.at[groups - 1 + r], group_recv.at[groups - 1 + r], device)
            )
            returned[-1].start()
        rows = pl.ds(at, sublength)
        local_out[rows, :] = mixing * l_own[rows, :] + (1.0 - mixing) * anchor_next

    def outer_second():
        for r, copy in enumerate(returned):
            copy.wait_recv()
            source = lax.rem(group + groups - 1 - r, groups)
            rows = pl.ds(pl.multiple_of(source * sublength, sublength), sublength)
            local_out[rows, :] = mixing * l_own[rows, :] + (1.0 - mixing) * a_in[r].astype(jnp.float32)

    run = {"dot": step_dot, "y1": step_y1, "z1": step_z1, "z2": step_z2, "y2": step_y2}
    for number, name in enumerate(ORDER):
        if number == len(ORDER) // 2:
            outer_first()
        if number == len(ORDER) * 3 // 4:
            outer_second()
        run[name[0]](*name[1:])

    grad_out[...] = jnp.transpose(fin[...])
    for copy in list(swaps.values()) + spread + returned + [copy for copy, _ in messages.values()]:
        copy.wait_send()


def reduced(hidden, cotangent, sync_frag, frag_local, frag_anchor, frag_momentum):
    tokens, keys = cotangent.shape[1:]
    frags, sublength, _ = frag_anchor.shape
    rows = frag_local.shape[1]
    groups = lax.axis_size("group")
    pairs, blocks = len(PAIRS), len(SLOT)
    bf16, f32 = jnp.bfloat16, jnp.float32
    half1, half2 = (H1, R1 - H1), (H2, keys - R1 - H2)
    n1, n2 = R1, keys - R1
    messages = 2 * (16 + 2 + 16 + 4)
    vmem = pl.BlockSpec(memory_space=pltpu.VMEM)
    hbm = pl.BlockSpec(memory_space=pltpu.HBM)
    stay = lambda x: pltpu.with_memory_space_constraint(x, pltpu.HBM)
    return pl.pallas_call(
        kernel,
        out_shape=(
            jax.ShapeDtypeStruct((rows, keys), f32),
            jax.ShapeDtypeStruct((rows, keys), f32),
            jax.ShapeDtypeStruct((sublength, keys), f32),
            jax.ShapeDtypeStruct((sublength, keys), f32),
        ),
        in_specs=[hbm, hbm, pl.BlockSpec(memory_space=pltpu.SMEM), hbm, hbm, hbm],
        out_specs=(vmem, vmem, vmem, vmem),
        scratch_shapes=[
            pltpu.VMEM((pairs, tokens, 2 * LANES), bf16),
            pltpu.VMEM((pairs, tokens, 2 * LANES), bf16),
            pltpu.VMEM((tokens, keys), bf16),
            pltpu.VMEM((tokens, keys), bf16),
            pltpu.VMEM((2, keys, tokens), bf16),
            pltpu.VMEM((pairs, keys, 2 * LANES), f32),
            pltpu.VMEM((keys, LANES), f32),
            pltpu.VMEM((2, NZ, half1[0], LANES), bf16),
            pltpu.VMEM((2, NZ, half1[1], LANES), bf16),
            pltpu.VMEM((2, 2, NY // 2 - 1, NZ, n1, LANES), bf16),
            pltpu.VMEM((2, half1[0], LANES), bf16),
            pltpu.VMEM((2, half1[1], LANES), bf16),
            pltpu.VMEM((2, 2, n1, LANES), bf16),
            pltpu.VMEM((2, NY, half2[0], LANES), bf16),
            pltpu.VMEM((2, NY, half2[1], LANES), bf16),
            pltpu.VMEM((2, 2, NY, n2, LANES), bf16),
            pltpu.VMEM((2, half2[0], LANES), bf16),
            pltpu.VMEM((2, half2[1], LANES), bf16),
            pltpu.VMEM((2, 2, NY // 2 - 1, n2, LANES), bf16),
            pltpu.VMEM((rows, keys), f32),
            pltpu.VMEM((groups - 1, sublength, keys), f32),
            pltpu.VMEM((frags, sublength, keys), f32),
            pltpu.VMEM((frags, sublength, keys), f32),
            pltpu.VMEM((sublength, keys), bf16),
            pltpu.VMEM((groups - 1, sublength, keys), bf16),
            pltpu.SemaphoreType.DMA((blocks + 4,)),
            pltpu.SemaphoreType.DMA((blocks + 1,)),
            pltpu.SemaphoreType.DMA((blocks + 1,)),
            pltpu.SemaphoreType.DMA((messages,)),
            pltpu.SemaphoreType.DMA((messages,)),
            pltpu.SemaphoreType.DMA((2 * (groups - 1),)),
            pltpu.SemaphoreType.DMA((2 * (groups - 1),)),
        ],
        compiler_params=pltpu.CompilerParams(
            collective_id=0, has_side_effects=True, vmem_limit_bytes=40 * 1024 * 1024
        ),
        name="reduce_and_sync",
    )(stay(hidden), stay(cotangent), sync_frag, stay(frag_local), stay(frag_anchor), stay(frag_momentum))


def finish(
    gradient, weight, first, second, local, anchor, momentum,
    weight_out, first_out, second_out, local_out, anchor_out, momentum_out,
):
    slope = gradient[...]
    moment_one = beta_one * first[0].astype(jnp.float32) + (1.0 - beta_one) * slope
    moment_two = beta_two * second[0].astype(jnp.float32) + (1.0 - beta_two) * slope * slope
    step_size = moment_one / bias_one / (jnp.sqrt(moment_two / bias_two) + epsilon)
    master = weight[0]
    weight_out[0] = master - inner_rate * (step_size + weight_decay * master)
    first_out[0] = moment_one.astype(jnp.bfloat16)
    second_out[0] = moment_two.astype(jnp.bfloat16)
    local_out[0] = local[...]
    anchor_out[...] = anchor[...]
    momentum_out[...] = momentum[...]


def finished(gradient, weight, first, second, local, anchor, momentum):
    vmem = pl.BlockSpec(memory_space=pltpu.VMEM)
    shape = jax.ShapeDtypeStruct
    return pl.pallas_call(
        finish,
        out_shape=(
            shape(weight.shape, weight.dtype),
            shape(first.shape, first.dtype),
            shape(second.shape, second.dtype),
            shape(weight.shape, local.dtype),
            shape(anchor.shape, anchor.dtype),
            shape(momentum.shape, momentum.dtype),
        ),
        in_specs=[vmem] * 7,
        out_specs=(vmem,) * 6,
        compiler_params=pltpu.CompilerParams(vmem_limit_bytes=16 * 1024 * 1024),
        name="finish",
    )(gradient, weight, first, second, local, anchor, momentum)


def per_device(
    hidden,
    cotangent,
    weight,
    first_moment,
    second_moment,
    sync_frag,
    frag_local,
    frag_anchor,
    frag_momentum,
):
    gradient, new_local, anchor_out, momentum_out = reduced(
        hidden, cotangent, sync_frag, frag_local, frag_anchor, frag_momentum
    )
    return finished(
        gradient, weight, first_moment, second_moment, new_local, anchor_out, momentum_out
    )


def solution(mesh):
    in_specs = (
        P("group", "fsdp", None),
        P("group", "fsdp", None),
        P("group", "fsdp", None),
        P("group", "fsdp", None),
        P("group", "fsdp", None),
        P(),
        P("group", "fsdp", None),
        P(None, ("fsdp", "group"), None),
        P(None, ("fsdp", "group"), None),
    )
    out_specs = (
        P("group", "fsdp", None),
        P("group", "fsdp", None),
        P("group", "fsdp", None),
        P("group", "fsdp", None),
        P(("fsdp", "group"), None),
        P(("fsdp", "group"), None),
    )
    return jax.shard_map(
        per_device, mesh=mesh, in_specs=in_specs, out_specs=out_specs, check_vma=False
    )
```

```python
import jax
import jax.numpy as jnp
from jax import lax
from jax.experimental import pallas as pl
from jax.experimental.pallas import tpu as pltpu
from jax.sharding import PartitionSpec as P

beta_one = 0.9
beta_two = 0.95
bias_one = 1.0 - 0.9**10
bias_two = 1.0 - 0.95**10
inner_rate = 0.01
weight_decay = 0.1
epsilon = 1e-08
outer_rate = 0.7
outer_mu = 0.9
mixing = 0.5

NY, NZ, NC = 8, 4, 2
DYS = (4, 3, -3, 2, -2, 1, -1, 0)
DZS = (2, 1, -1, 0)
UP, DOWN = 0, 1
SIGN = (1, -1)
R1 = 352
H1 = 176
H2 = 80
LANES = 128
Y_FIRST = ((0,), (1,), (2,), (3,))
Z_FIRST = ((0,), (1, 2), (3, 4), (5, 6, 7))


PAIRS = (
    (((4, 2), (4, 1)), ((4, -1), (4, 0)))
    + tuple(((dy, 2), (-dy, 2)) for dy in (3, 2, 1))
    + (((0, 2), (0, 0)),)
    + tuple(((dy, 1), (dy, -1)) for dy in (3, -3, 2, -2, 1, -1, 0))
    + tuple(((dy, 0), (-dy, 0)) for dy in (3, 2, 1))
)
SLOT = {block: (i, j) for i, pair in enumerate(PAIRS) for j, block in enumerate(pair)}

ORDER = (
    ("dot", 0), ("y0", 0, 1), ("y0", 0, 0), ("z2", 0, 0, 1), ("dot", 1), ("y0", 1, 0), ("z2", 0, 0, 0),
    ("y0", 2, 1), ("y0", 2, 0), ("dot", 3), ("z2", 2, 0, 1), ("y0", 3, 1), ("z2", 2, 0, 0), ("dot", 7),
    ("y0", 3, 0), ("dot", 10), ("dot", 2), ("y0", 1, 1), ("dot", 6), ("dot", 13), ("y1", 0, 1, 1),
    ("y1", 0, 1, 0), ("dot", 4), ("z2", 1, 0, 1), ("z2", 1, 0, 0), ("dot", 8), ("y1", 2, 1, 1), ("dot", 5),
    ("dot", 9), ("y1", 1, 1, 0), ("z2", 0, 1, 1), ("z2", 0, 1, 0), ("y1", 1, 1, 1), ("dot", 12),
    ("y1", 2, 1, 0), ("z2", 3, 0, 0), ("z2", 3, 0, 1), ("y1", 0, 2, 1), ("y1", 0, 2, 0), ("y1", 1, 2, 0),
    ("z2", 2, 1, 1), ("z2", 1, 1, 0), ("y1", 2, 2, 1), ("y2", 0, 0), ("y2", 0, 1), ("z2", 1, 1, 1),
    ("y1", 0, 3, 1), ("y1", 0, 3, 0), ("dot", 15), ("y1", 1, 2, 1), ("y1", 2, 2, 0), ("dot", 14),
    ("z2", 2, 1, 0), ("dot", 11), ("y1", 3, 1, 0), ("y1", 2, 3, 1), ("y1", 1, 3, 0), ("y1", 3, 1, 1),
    ("z1", 0, 0), ("y1", 1, 3, 1), ("z2", 3, 1, 0), ("z2", 3, 1, 1), ("y1", 2, 3, 0), ("y2", 1, 0),
    ("y2", 1, 1), ("y1", 3, 2, 0), ("y1", 3, 2, 1), ("z1", 1, 0), ("z1", 1, 1), ("y2", 2, 0), ("y2", 2, 1),
    ("y1", 3, 3, 1), ("y1", 3, 3, 0), ("y2", 3, 0), ("y2", 3, 1), ("y2", 4), ("z1", 2),
)


def kernel(
    hid, cot, chosen, local, anchor, mom,
    grad_out, local_out, anchor_out, mom_out,
    h_own, h_peer, c_own, c_peer, ct, part, fin,
    y1a, y1b, y1w, z1a, z1b, z1w, z2a, z2b, z2w, y2a, y2b, y2w,
    l_own, l_in, a_all, m_all, a_send, a_in,
    load_sem, peer_send, peer_recv, send_sem, recv_sem, group_send, group_recv,
):
    group = lax.axis_index("group")
    me = lax.axis_index("fsdp")
    groups = lax.axis_size("group")
    y, z, core = me // (NZ * NC), (me // NC) % NZ, me % NC
    place = lambda yy, zz, cc: (lax.rem(yy + NY, NY) * NZ + lax.rem(zz + NZ, NZ)) * NC + cc
    peer = (group, place(y, z, 1 - core))
    partner = {
        "y": [(group, place(y + sign, z, core)) for sign in SIGN],
        "z": [(group, place(y, z + sign, core)) for sign in SIGN],
    }
    members = [(lax.rem(group + r, groups), me) for r in range(1, groups)]
    sublength = anchor.shape[1]

    barrier = pltpu.get_barrier_semaphore()
    everyone = [peer] + partner["y"] + partner["z"] + members
    for device in everyone:
        pl.semaphore_signal(barrier, inc=1, device_id=device, device_id_type=pl.DeviceIdType.MESH)

    loads = {}

    def load(name, source, target):
        loads[name] = pltpu.make_async_copy(source, target, load_sem.at[len(loads)])
        loads[name].start()

    def columns(block, cc):
        at = pl.multiple_of(place(y + block[0], z + block[1], cc) * LANES, LANES)
        return hid.at[0, :, pl.ds(at, LANES)]

    def half(ref, block):
        i, j = SLOT[block]
        return ref.at[i, :, j * LANES : (j + 1) * LANES]

    def remote(source, target, send, recv, device):
        return pltpu.make_async_remote_copy(
            src_ref=source, dst_ref=target, send_sem=send, recv_sem=recv,
            device_id=device, device_id_type=pl.DeviceIdType.MESH,
        )

    swaps = {}

    def swap(name, source, target):
        number = len(swaps)
        swaps[name] = remote(source, target, peer_send.at[number], peer_recv.at[number], peer)
        swaps[name].start()

    def swap_blocks(blocks):
        for block in blocks:
            swap(block, columns(block, 1 - core), half(h_peer, block))

    def load_blocks(blocks):
        for block in blocks:
            load(block, columns(block, core), half(h_own, block))

    blocks = list(SLOT)
    load("cot", cot.at[0], c_own)
    pl.semaphore_wait(barrier, len(everyone))
    swap("cot", cot.at[0], c_peer)
    swap_blocks(blocks)
    load_blocks(blocks)
    load("local", local.at[0], l_own)
    load("anchor", anchor, a_all)
    load("mom", mom, m_all)
    spread = []
    for r, device in enumerate(members):
        rows = pl.ds(pl.multiple_of(device[0] * sublength, sublength), sublength)
        spread.append(
            remote(local.at[0, rows], l_in.at[r], group_send.at[r], group_recv.at[r], device)
        )
        spread[-1].start()
    loads["cot"].wait()
    ct[0] = jnp.transpose(c_own[...].astype(jnp.float32)).astype(jnp.bfloat16)
    swaps["cot"].wait_recv()
    ct[1] = jnp.transpose(c_peer[...].astype(jnp.float32)).astype(jnp.bfloat16)

    copies, messages, landed = [], {}, set()

    def depart(axis, d, out, into):
        number = len(copies)
        copies.append(remote(out, into, send_sem.at[number], recv_sem.at[number], partner[axis][d]))
        copies[-1].start()
        return number

    def send(name, axis, d, bufs, index, value):
        out, into = bufs.at[(0,) + index], bufs.at[(1,) + index]
        out[...] = value.astype(jnp.bfloat16)
        messages[name] = (depart(axis, d, out, into), into)

    def send_strips(names, axis, d, bufs, index, strips, values):
        for strip, value in zip(strips, values):
            bufs[(0,) + index + (strip,)] = value.astype(jnp.bfloat16)
        side = (pl.ds(strips[0], len(strips)),)
        number = depart(axis, d, bufs.at[(0,) + index + side], bufs.at[(1,) + index + side])
        for name, strip in zip(names, strips):
            messages[name] = (number, bufs.at[(1,) + index + (strip,)])

    def arrived(name):
        number, into = messages[name]
        if number not in landed:
            landed.add(number)
            copies[number].wait_recv()
        return into[...].astype(jnp.float32)

    def own(dy, dz, begin, end):
        i, j = SLOT[dy, dz]
        return part[i, begin:end, j * LANES : (j + 1) * LANES]

    def with_part(name, d, whole, cut):
        came = arrived(name)
        if d == UP:
            return jnp.concatenate([whole[:cut] + came, whole[cut:]], axis=0)
        return jnp.concatenate([whole[:cut], whole[cut:] + came], axis=0)

    def step_dot(i):
        for block in PAIRS[i]:
            loads[block].wait()
            swaps[block].wait_recv()
        part[i] = jnp.dot(ct[0], h_own[i], preferred_element_type=jnp.float32) + jnp.dot(
            ct[1], h_peer[i], preferred_element_type=jnp.float32
        )

    def step_y0(group, d):
        begin, end = ((0, H1), (H1, R1))[d]
        strips = Y_FIRST[group]
        send_strips(
            [("y1", s, 0, d) for s in strips], "y", d, (y1a, y1b)[d], (), strips,
            [own(4, DZS[s], begin, end) for s in strips],
        )

    def step_y1(s, h, d):
        dz = DZS[s]
        whole = own(SIGN[d] * (4 - h), dz, 0, R1)
        if h == 1:
            whole = with_part(("y1", s, 0, d), d, whole, H1)
        else:
            whole = whole + arrived(("y1", s, h - 1, d))
        send(("y1", s, h, d), "y", d, y1w, (d, h - 1, s), whole)

    def y1_sum(s):
        return own(0, DZS[s], 0, R1) + arrived(("y1", s, 3, UP)) + arrived(("y1", s, 3, DOWN))

    def step_z1(h, d=None):
        if h == 0:
            whole = y1_sum(0)
            send(("z1", 0, UP), "z", UP, z1a, (), whole[:H1])
            send(("z1", 0, DOWN), "z", DOWN, z1b, (), whole[H1:])
        elif h == 1:
            whole = with_part(("z1", 0, d), d, y1_sum(1 + d), H1)
            send(("z1", 1, d), "z", d, z1w, (d,), whole)
        else:
            fin[0:R1, :] = y1_sum(3) + arrived(("z1", 1, UP)) + arrived(("z1", 1, DOWN))

    def step_z2(group, h, d):
        strips = Z_FIRST[group]
        names = [("z2", k, h, d) for k in strips]
        if h == 0:
            begin, end = ((R1, R1 + H2), (R1 + H2, 512))[d]
            values = [own(DYS[k], 2, begin, end) for k in strips]
            send_strips(names, "z", d, (z2a, z2b)[d], (), strips, values)
            return
        values = [with_part(("z2", k, 0, d), d, own(DYS[k], SIGN[d], R1, 512), H2) for k in strips]
        send_strips(names, "z", d, z2w, (d,), strips, values)

    def z2_sum(k):
        return own(DYS[k], 0, R1, 512) + arrived(("z2", k, 1, UP)) + arrived(("z2", k, 1, DOWN))

    far = []

    def step_y2(h, d=None):
        if h == 0:
            if not far:
                far.append(z2_sum(0))
            value = far[0][:H2] if d == UP else far[0][H2:]
            send(("y2", 0, d), "y", d, (y2a, y2b)[d], (), value)
        elif h < 4:
            whole = z2_sum(2 * h - 1 + d)
            if h == 1:
                whole = with_part(("y2", 0, d), d, whole, H2)
            else:
                whole = whole + arrived(("y2", h - 1, d))
            send(("y2", h, d), "y", d, y2w, (d, h - 1), whole)
        else:
            fin[R1:512, :] = z2_sum(7) + arrived(("y2", 3, UP)) + arrived(("y2", 3, DOWN))

    returned = []

    def outer_first():
        for name in ("local", "anchor", "mom"):
            loads[name].wait()
        at = pl.multiple_of(group * sublength, sublength)
        total = l_own[pl.ds(at, sublength), :]
        for r, copy in enumerate(spread):
            copy.wait_recv()
            total = total + l_in[r]
        f = chosen[0]
        here = a_all[f]
        mean_delta = here - total * (1.0 / groups)
        momentum_next = outer_mu * m_all[f] + mean_delta
        anchor_next = here - outer_rate * (mean_delta + outer_mu * momentum_next)
        anchor_out[...] = anchor_next
        mom_out[...] = momentum_next
        a_send[...] = anchor_next.astype(jnp.bfloat16)
        for r, device in enumerate(members):
            returned.append(
                remote(a_send, a_in.at[r], group_send.at[groups - 1 + r], group_recv.at[groups - 1 + r], device)
            )
            returned[-1].start()
        rows = pl.ds(at, sublength)
        local_out[rows, :] = mixing * l_own[rows, :] + (1.0 - mixing) * anchor_next

    def outer_second():
        for r, copy in enumerate(returned):
            copy.wait_recv()
            source = lax.rem(group + groups - 1 - r, groups)
            rows = pl.ds(pl.multiple_of(source * sublength, sublength), sublength)
            local_out[rows, :] = mixing * l_own[rows, :] + (1.0 - mixing) * a_in[r].astype(jnp.float32)

    run = {"dot": step_dot, "y0": step_y0, "y1": step_y1, "z1": step_z1, "z2": step_z2, "y2": step_y2}
    for number, name in enumerate(ORDER):
        if number == len(ORDER) // 2:
            outer_first()
        if number == len(ORDER) * 3 // 4:
            outer_second()
        run[name[0]](*name[1:])

    grad_out[...] = jnp.transpose(fin[...])
    for copy in list(swaps.values()) + spread + returned + copies:
        copy.wait_send()


def reduced(hidden, cotangent, sync_frag, frag_local, frag_anchor, frag_momentum):
    tokens, keys = cotangent.shape[1:]
    frags, sublength, _ = frag_anchor.shape
    rows = frag_local.shape[1]
    groups = lax.axis_size("group")
    pairs, blocks = len(PAIRS), len(SLOT)
    bf16, f32 = jnp.bfloat16, jnp.float32
    half1, half2 = (H1, R1 - H1), (H2, keys - R1 - H2)
    n1, n2 = R1, keys - R1
    messages = 2 * (16 + 2 + 16 + 4)
    vmem = pl.BlockSpec(memory_space=pltpu.VMEM)
    hbm = pl.BlockSpec(memory_space=pltpu.HBM)
    stay = lambda x: pltpu.with_memory_space_constraint(x, pltpu.HBM)
    return pl.pallas_call(
        kernel,
        out_shape=(
            jax.ShapeDtypeStruct((rows, keys), f32),
            jax.ShapeDtypeStruct((rows, keys), f32),
            jax.ShapeDtypeStruct((sublength, keys), f32),
            jax.ShapeDtypeStruct((sublength, keys), f32),
        ),
        in_specs=[hbm, hbm, pl.BlockSpec(memory_space=pltpu.SMEM), hbm, hbm, hbm],
        out_specs=(vmem, vmem, vmem, vmem),
        scratch_shapes=[
            pltpu.VMEM((pairs, tokens, 2 * LANES), bf16),
            pltpu.VMEM((pairs, tokens, 2 * LANES), bf16),
            pltpu.VMEM((tokens, keys), bf16),
            pltpu.VMEM((tokens, keys), bf16),
            pltpu.VMEM((2, keys, tokens), bf16),
            pltpu.VMEM((pairs, keys, 2 * LANES), f32),
            pltpu.VMEM((keys, LANES), f32),
            pltpu.VMEM((2, NZ, half1[0], LANES), bf16),
            pltpu.VMEM((2, NZ, half1[1], LANES), bf16),
            pltpu.VMEM((2, 2, NY // 2 - 1, NZ, n1, LANES), bf16),
            pltpu.VMEM((2, half1[0], LANES), bf16),
            pltpu.VMEM((2, half1[1], LANES), bf16),
            pltpu.VMEM((2, 2, n1, LANES), bf16),
            pltpu.VMEM((2, NY, half2[0], LANES), bf16),
            pltpu.VMEM((2, NY, half2[1], LANES), bf16),
            pltpu.VMEM((2, 2, NY, n2, LANES), bf16),
            pltpu.VMEM((2, half2[0], LANES), bf16),
            pltpu.VMEM((2, half2[1], LANES), bf16),
            pltpu.VMEM((2, 2, NY // 2 - 1, n2, LANES), bf16),
            pltpu.VMEM((rows, keys), f32),
            pltpu.VMEM((groups - 1, sublength, keys), f32),
            pltpu.VMEM((frags, sublength, keys), f32),
            pltpu.VMEM((frags, sublength, keys), f32),
            pltpu.VMEM((sublength, keys), bf16),
            pltpu.VMEM((groups - 1, sublength, keys), bf16),
            pltpu.SemaphoreType.DMA((blocks + 4,)),
            pltpu.SemaphoreType.DMA((blocks + 1,)),
            pltpu.SemaphoreType.DMA((blocks + 1,)),
            pltpu.SemaphoreType.DMA((messages,)),
            pltpu.SemaphoreType.DMA((messages,)),
            pltpu.SemaphoreType.DMA((2 * (groups - 1),)),
            pltpu.SemaphoreType.DMA((2 * (groups - 1),)),
        ],
        compiler_params=pltpu.CompilerParams(
            collective_id=0, has_side_effects=True, vmem_limit_bytes=40 * 1024 * 1024
        ),
        name="reduce_and_sync",
    )(stay(hidden), stay(cotangent), sync_frag, stay(frag_local), stay(frag_anchor), stay(frag_momentum))


def finish(
    gradient, weight, first, second, local, anchor, momentum,
    weight_out, first_out, second_out, local_out, anchor_out, momentum_out,
):
    slope = gradient[...]
    moment_one = beta_one * first[0].astype(jnp.float32) + (1.0 - beta_one) * slope
    moment_two = beta_two * second[0].astype(jnp.float32) + (1.0 - beta_two) * slope * slope
    step_size = moment_one / bias_one / (jnp.sqrt(moment_two / bias_two) + epsilon)
    master = weight[0]
    weight_out[0] = master - inner_rate * (step_size + weight_decay * master)
    first_out[0] = moment_one.astype(jnp.bfloat16)
    second_out[0] = moment_two.astype(jnp.bfloat16)
    local_out[0] = local[...]
    anchor_out[...] = anchor[...]
    momentum_out[...] = momentum[...]


def finished(gradient, weight, first, second, local, anchor, momentum):
    vmem = pl.BlockSpec(memory_space=pltpu.VMEM)
    shape = jax.ShapeDtypeStruct
    return pl.pallas_call(
        finish,
        out_shape=(
            shape(weight.shape, weight.dtype),
            shape(first.shape, first.dtype),
            shape(second.shape, second.dtype),
            shape(weight.shape, local.dtype),
            shape(anchor.shape, anchor.dtype),
            shape(momentum.shape, momentum.dtype),
        ),
        in_specs=[vmem] * 7,
        out_specs=(vmem,) * 6,
        compiler_params=pltpu.CompilerParams(vmem_limit_bytes=16 * 1024 * 1024),
        name="finish",
    )(gradient, weight, first, second, local, anchor, momentum)


def per_device(
    hidden,
    cotangent,
    weight,
    first_moment,
    second_moment,
    sync_frag,
    frag_local,
    frag_anchor,
    frag_momentum,
):
    gradient, new_local, anchor_out, momentum_out = reduced(
        hidden, cotangent, sync_frag, frag_local, frag_anchor, frag_momentum
    )
    return finished(
        gradient, weight, first_moment, second_moment, new_local, anchor_out, momentum_out
    )


def solution(mesh):
    in_specs = (
        P("group", "fsdp", None),
        P("group", "fsdp", None),
        P("group", "fsdp", None),
        P("group", "fsdp", None),
        P("group", "fsdp", None),
        P(),
        P("group", "fsdp", None),
        P(None, ("fsdp", "group"), None),
        P(None, ("fsdp", "group"), None),
    )
    out_specs = (
        P("group", "fsdp", None),
        P("group", "fsdp", None),
        P("group", "fsdp", None),
        P("group", "fsdp", None),
        P(("fsdp", "group"), None),
        P(("fsdp", "group"), None),
    )
    return jax.shard_map(
        per_device, mesh=mesh, in_specs=in_specs, out_specs=out_specs, check_vma=False
    )
```

```python
import jax
import jax.numpy as jnp
from jax import lax
from jax.experimental import pallas as pl
from jax.experimental.pallas import tpu as pltpu
from jax.sharding import PartitionSpec as P

beta_one = 0.9
beta_two = 0.95
bias_one = 1.0 - 0.9**10
bias_two = 1.0 - 0.95**10
inner_rate = 0.01
weight_decay = 0.1
epsilon = 1e-08
outer_rate = 0.7
outer_mu = 0.9
mixing = 0.5

NY, NZ, NC = 8, 4, 2
DYS = (4, 3, -3, 2, -2, 1, -1, 0)
DZS = (2, 1, -1, 0)
UP, DOWN = 0, 1
SIGN = (1, -1)
R1 = 352
H1 = 176
H2 = 80
LANES = 128
Y_FIRST = ((0,), (1,), (2,), (3,))
Z_FIRST = ((0,), (1, 2), (3, 4), (5, 6, 7))


PAIRS = (
    (((4, 2), (4, 1)), ((4, -1), (4, 0)))
    + tuple(((dy, 2), (-dy, 2)) for dy in (3, 2, 1))
    + (((0, 2), (0, 0)),)
    + tuple(((dy, 1), (dy, -1)) for dy in (3, -3, 2, -2, 1, -1, 0))
    + tuple(((dy, 0), (-dy, 0)) for dy in (3, 2, 1))
)
SLOT = {block: (i, j) for i, pair in enumerate(PAIRS) for j, block in enumerate(pair)}

ORDER = (
    ("dot", 0), ("y0", 0, 1), ("y0", 0, 0), ("z2", 0, 0, 1), ("dot", 1), ("y0", 1, 0), ("z2", 0, 0, 0),
    ("y0", 2, 1), ("y0", 2, 0), ("dot", 3), ("z2", 2, 0, 1), ("y0", 3, 1), ("z2", 2, 0, 0), ("dot", 7),
    ("y0", 3, 0), ("dot", 10), ("dot", 2), ("y0", 1, 1), ("dot", 6), ("dot", 13), ("y1", 0, 1, 1),
    ("y1", 0, 1, 0), ("dot", 4), ("z2", 1, 0, 1), ("z2", 1, 0, 0), ("dot", 8), ("y1", 2, 1, 1), ("dot", 5),
    ("dot", 9), ("y1", 1, 1, 0), ("z2", 0, 1, 1), ("z2", 0, 1, 0), ("y1", 1, 1, 1), ("dot", 12),
    ("y1", 2, 1, 0), ("z2", 3, 0, 0), ("z2", 3, 0, 1), ("y1", 0, 2, 1), ("y1", 0, 2, 0), ("y1", 1, 2, 0),
    ("z2", 2, 1, 1), ("z2", 1, 1, 0), ("y1", 2, 2, 1), ("y2", 0, 0), ("y2", 0, 1), ("z2", 1, 1, 1),
    ("y1", 0, 3, 1), ("y1", 0, 3, 0), ("dot", 15), ("y1", 1, 2, 1), ("y1", 2, 2, 0), ("dot", 14),
    ("z2", 2, 1, 0), ("dot", 11), ("y1", 3, 1, 0), ("y1", 2, 3, 1), ("y1", 1, 3, 0), ("y1", 3, 1, 1),
    ("z1", 0, 0), ("y1", 1, 3, 1), ("z2", 3, 1, 0), ("z2", 3, 1, 1), ("y1", 2, 3, 0), ("y2", 1, 0),
    ("y2", 1, 1), ("y1", 3, 2, 0), ("y1", 3, 2, 1), ("z1", 1, 0), ("z1", 1, 1), ("y2", 2, 0), ("y2", 2, 1),
    ("y1", 3, 3, 1), ("y1", 3, 3, 0), ("y2", 3, 0), ("y2", 3, 1), ("y2", 4), ("z1", 2),
)


def kernel(
    hid, cot, chosen, local, anchor, mom,
    grad_out, local_out, anchor_out, mom_out,
    h_own, h_peer, c_own, c_peer, ct, part, fin,
    y1a, y1b, y1w, z1a, z1b, z1w, z2a, z2b, z2w, y2a, y2b, y2w,
    l_own, l_in, a_all, m_all, a_send, a_in,
    load_sem, peer_send, peer_recv, send_sem, recv_sem, group_send, group_recv,
):
    group = lax.axis_index("group")
    me = lax.axis_index("fsdp")
    groups = lax.axis_size("group")
    y, z, core = me // (NZ * NC), (me // NC) % NZ, me % NC
    place = lambda yy, zz, cc: (lax.rem(yy + NY, NY) * NZ + lax.rem(zz + NZ, NZ)) * NC + cc
    peer = (group, place(y, z, 1 - core))
    partner = {
        "y": [(group, place(y + sign, z, core)) for sign in SIGN],
        "z": [(group, place(y, z + sign, core)) for sign in SIGN],
    }
    members = [(lax.rem(group + r, groups), me) for r in range(1, groups)]
    sublength = anchor.shape[1]

    barrier = pltpu.get_barrier_semaphore()
    everyone = [peer] + partner["y"] + partner["z"] + members
    for device in everyone:
        pl.semaphore_signal(barrier, inc=1, device_id=device, device_id_type=pl.DeviceIdType.MESH)

    loads = {}

    def load(name, source, target):
        loads[name] = pltpu.make_async_copy(source, target, load_sem.at[len(loads)])
        loads[name].start()

    def columns(block, cc):
        at = pl.multiple_of(place(y + block[0], z + block[1], cc) * LANES, LANES)
        return hid.at[0, :, pl.ds(at, LANES)]

    def half(ref, block):
        i, j = SLOT[block]
        return ref.at[i, :, j * LANES : (j + 1) * LANES]

    def remote(source, target, send, recv, device):
        return pltpu.make_async_remote_copy(
            src_ref=source, dst_ref=target, send_sem=send, recv_sem=recv,
            device_id=device, device_id_type=pl.DeviceIdType.MESH,
        )

    swaps = {}

    def swap(name, source, target):
        number = len(swaps)
        swaps[name] = remote(source, target, peer_send.at[number], peer_recv.at[number], peer)
        swaps[name].start()

    def swap_blocks(blocks):
        for block in blocks:
            swap(block, columns(block, 1 - core), half(h_peer, block))

    def load_blocks(blocks):
        for block in blocks:
            load(block, columns(block, core), half(h_own, block))

    blocks = list(SLOT)
    load("cot", cot.at[0], c_own)
    pl.semaphore_wait(barrier, len(everyone))
    swap("cot", cot.at[0], c_peer)
    swap_blocks(blocks)
    load_blocks(blocks)
    load("local", local.at[0], l_own)
    load("anchor", anchor, a_all)
    load("mom", mom, m_all)
    spread = []
    for r, device in enumerate(members):
        rows = pl.ds(pl.multiple_of(device[0] * sublength, sublength), sublength)
        spread.append(
            remote(local.at[0, rows], l_in.at[r], group_send.at[r], group_recv.at[r], device)
        )
        spread[-1].start()
    loads["cot"].wait()
    ct[0] = jnp.transpose(c_own[...].astype(jnp.float32)).astype(jnp.bfloat16)
    swaps["cot"].wait_recv()
    ct[1] = jnp.transpose(c_peer[...].astype(jnp.float32)).astype(jnp.bfloat16)

    copies, messages, landed = [], {}, set()

    def depart(axis, d, out, into):
        number = len(copies)
        copies.append(remote(out, into, send_sem.at[number], recv_sem.at[number], partner[axis][d]))
        copies[-1].start()
        return number

    def send(name, axis, d, bufs, index, value):
        out, into = bufs.at[(0,) + index], bufs.at[(1,) + index]
        out[...] = value.astype(jnp.bfloat16)
        messages[name] = (depart(axis, d, out, into), into)

    def send_strips(names, axis, d, bufs, index, strips, values):
        for strip, value in zip(strips, values):
            bufs[(0,) + index + (strip,)] = value.astype(jnp.bfloat16)
        side = (pl.ds(strips[0], len(strips)),)
        number = depart(axis, d, bufs.at[(0,) + index + side], bufs.at[(1,) + index + side])
        for name, strip in zip(names, strips):
            messages[name] = (number, bufs.at[(1,) + index + (strip,)])

    def arrived(name):
        number, into = messages[name]
        if number not in landed:
            landed.add(number)
            copies[number].wait_recv()
        return into[...].astype(jnp.float32)

    def own(dy, dz, begin, end):
        i, j = SLOT[dy, dz]
        return part[i, begin:end, j * LANES : (j + 1) * LANES]

    def with_part(name, d, whole, cut):
        came = arrived(name)
        if d == UP:
            return jnp.concatenate([whole[:cut] + came, whole[cut:]], axis=0)
        return jnp.concatenate([whole[:cut], whole[cut:] + came], axis=0)

    def step_dot(i):
        for block in PAIRS[i]:
            loads[block].wait()
            swaps[block].wait_recv()
        part[i] = jnp.dot(ct[0], h_own[i], preferred_element_type=jnp.float32) + jnp.dot(
            ct[1], h_peer[i], preferred_element_type=jnp.float32
        )

    def step_y0(group, d):
        begin, end = ((0, H1), (H1, R1))[d]
        strips = Y_FIRST[group]
        send_strips(
            [("y1", s, 0, d) for s in strips], "y", d, (y1a, y1b)[d], (), strips,
            [own(4, DZS[s], begin, end) for s in strips],
        )

    def step_y1(s, h, d):
        dz = DZS[s]
        whole = own(SIGN[d] * (4 - h), dz, 0, R1)
        if h == 1:
            whole = with_part(("y1", s, 0, d), d, whole, H1)
        else:
            whole = whole + arrived(("y1", s, h - 1, d))
        send(("y1", s, h, d), "y", d, y1w, (d, h - 1, s), whole)

    def y1_sum(s):
        return own(0, DZS[s], 0, R1) + arrived(("y1", s, 3, UP)) + arrived(("y1", s, 3, DOWN))

    def step_z1(h, d=None):
        if h == 0:
            whole = y1_sum(0)
            send(("z1", 0, UP), "z", UP, z1a, (), whole[:H1])
            send(("z1", 0, DOWN), "z", DOWN, z1b, (), whole[H1:])
        elif h == 1:
            whole = y1_sum(1 + d)
            rows = ((0, H1), (H1, R1))
            for side in (1 - d, d):
                begin, end = rows[side]
                value = whole[begin:end]
                if side == d:
                    value = value + arrived(("z1", 0, d))
                place_of = (d, pl.ds(begin, end - begin))
                send(("z1", 1, d, side), "z", d, z1w, place_of, value)
        else:
            for side, (begin, end) in enumerate(((0, H1), (H1, R1))):
                fin[begin:end, :] = (
                    y1_sum(3)[begin:end] + arrived(("z1", 1, UP, side)) + arrived(("z1", 1, DOWN, side))
                )

    def step_z2(group, h, d):
        strips = Z_FIRST[group]
        names = [("z2", k, h, d) for k in strips]
        if h == 0:
            begin, end = ((R1, R1 + H2), (R1 + H2, 512))[d]
            values = [own(DYS[k], 2, begin, end) for k in strips]
            send_strips(names, "z", d, (z2a, z2b)[d], (), strips, values)
            return
        values = [with_part(("z2", k, 0, d), d, own(DYS[k], SIGN[d], R1, 512), H2) for k in strips]
        send_strips(names, "z", d, z2w, (d,), strips, values)

    def z2_sum(k):
        return own(DYS[k], 0, R1, 512) + arrived(("z2", k, 1, UP)) + arrived(("z2", k, 1, DOWN))

    far = []

    def step_y2(h, d=None):
        if h == 0:
            if not far:
                far.append(z2_sum(0))
            value = far[0][:H2] if d == UP else far[0][H2:]
            send(("y2", 0, d), "y", d, (y2a, y2b)[d], (), value)
        elif h < 4:
            whole = z2_sum(2 * h - 1 + d)
            if h == 1:
                whole = with_part(("y2", 0, d), d, whole, H2)
            else:
                whole = whole + arrived(("y2", h - 1, d))
            send(("y2", h, d), "y", d, y2w, (d, h - 1), whole)
        else:
            fin[R1:512, :] = z2_sum(7) + arrived(("y2", 3, UP)) + arrived(("y2", 3, DOWN))

    returned = []

    def outer_first():
        for name in ("local", "anchor", "mom"):
            loads[name].wait()
        at = pl.multiple_of(group * sublength, sublength)
        total = l_own[pl.ds(at, sublength), :]
        for r, copy in enumerate(spread):
            copy.wait_recv()
            total = total + l_in[r]
        f = chosen[0]
        here = a_all[f]
        mean_delta = here - total * (1.0 / groups)
        momentum_next = outer_mu * m_all[f] + mean_delta
        anchor_next = here - outer_rate * (mean_delta + outer_mu * momentum_next)
        anchor_out[...] = anchor_next
        mom_out[...] = momentum_next
        a_send[...] = anchor_next.astype(jnp.bfloat16)
        for r, device in enumerate(members):
            returned.append(
                remote(a_send, a_in.at[r], group_send.at[groups - 1 + r], group_recv.at[groups - 1 + r], device)
            )
            returned[-1].start()
        rows = pl.ds(at, sublength)
        local_out[rows, :] = mixing * l_own[rows, :] + (1.0 - mixing) * anchor_next

    def outer_second():
        for r, copy in enumerate(returned):
            copy.wait_recv()
            source = lax.rem(group + groups - 1 - r, groups)
            rows = pl.ds(pl.multiple_of(source * sublength, sublength), sublength)
            local_out[rows, :] = mixing * l_own[rows, :] + (1.0 - mixing) * a_in[r].astype(jnp.float32)

    run = {"dot": step_dot, "y0": step_y0, "y1": step_y1, "z1": step_z1, "z2": step_z2, "y2": step_y2}
    for number, name in enumerate(ORDER):
        if number == len(ORDER) // 2:
            outer_first()
        if number == len(ORDER) * 3 // 4:
            outer_second()
        run[name[0]](*name[1:])

    grad_out[...] = jnp.transpose(fin[...])
    for copy in list(swaps.values()) + spread + returned + copies:
        copy.wait_send()


def reduced(hidden, cotangent, sync_frag, frag_local, frag_anchor, frag_momentum):
    tokens, keys = cotangent.shape[1:]
    frags, sublength, _ = frag_anchor.shape
    rows = frag_local.shape[1]
    groups = lax.axis_size("group")
    pairs, blocks = len(PAIRS), len(SLOT)
    bf16, f32 = jnp.bfloat16, jnp.float32
    half1, half2 = (H1, R1 - H1), (H2, keys - R1 - H2)
    n1, n2 = R1, keys - R1
    messages = 2 * (16 + 2 + 16 + 4)
    vmem = pl.BlockSpec(memory_space=pltpu.VMEM)
    hbm = pl.BlockSpec(memory_space=pltpu.HBM)
    stay = lambda x: pltpu.with_memory_space_constraint(x, pltpu.HBM)
    return pl.pallas_call(
        kernel,
        out_shape=(
            jax.ShapeDtypeStruct((rows, keys), f32),
            jax.ShapeDtypeStruct((rows, keys), f32),
            jax.ShapeDtypeStruct((sublength, keys), f32),
            jax.ShapeDtypeStruct((sublength, keys), f32),
        ),
        in_specs=[hbm, hbm, pl.BlockSpec(memory_space=pltpu.SMEM), hbm, hbm, hbm],
        out_specs=(vmem, vmem, vmem, vmem),
        scratch_shapes=[
            pltpu.VMEM((pairs, tokens, 2 * LANES), bf16),
            pltpu.VMEM((pairs, tokens, 2 * LANES), bf16),
            pltpu.VMEM((tokens, keys), bf16),
            pltpu.VMEM((tokens, keys), bf16),
            pltpu.VMEM((2, keys, tokens), bf16),
            pltpu.VMEM((pairs, keys, 2 * LANES), f32),
            pltpu.VMEM((keys, LANES), f32),
            pltpu.VMEM((2, NZ, half1[0], LANES), bf16),
            pltpu.VMEM((2, NZ, half1[1], LANES), bf16),
            pltpu.VMEM((2, 2, NY // 2 - 1, NZ, n1, LANES), bf16),
            pltpu.VMEM((2, half1[0], LANES), bf16),
            pltpu.VMEM((2, half1[1], LANES), bf16),
            pltpu.VMEM((2, 2, n1, LANES), bf16),
            pltpu.VMEM((2, NY, half2[0], LANES), bf16),
            pltpu.VMEM((2, NY, half2[1], LANES), bf16),
            pltpu.VMEM((2, 2, NY, n2, LANES), bf16),
            pltpu.VMEM((2, half2[0], LANES), bf16),
            pltpu.VMEM((2, half2[1], LANES), bf16),
            pltpu.VMEM((2, 2, NY // 2 - 1, n2, LANES), bf16),
            pltpu.VMEM((rows, keys), f32),
            pltpu.VMEM((groups - 1, sublength, keys), f32),
            pltpu.VMEM((frags, sublength, keys), f32),
            pltpu.VMEM((frags, sublength, keys), f32),
            pltpu.VMEM((sublength, keys), bf16),
            pltpu.VMEM((groups - 1, sublength, keys), bf16),
            pltpu.SemaphoreType.DMA((blocks + 4,)),
            pltpu.SemaphoreType.DMA((blocks + 1,)),
            pltpu.SemaphoreType.DMA((blocks + 1,)),
            pltpu.SemaphoreType.DMA((messages,)),
            pltpu.SemaphoreType.DMA((messages,)),
            pltpu.SemaphoreType.DMA((2 * (groups - 1),)),
            pltpu.SemaphoreType.DMA((2 * (groups - 1),)),
        ],
        compiler_params=pltpu.CompilerParams(
            collective_id=0, has_side_effects=True, vmem_limit_bytes=40 * 1024 * 1024
        ),
        name="reduce_and_sync",
    )(stay(hidden), stay(cotangent), sync_frag, stay(frag_local), stay(frag_anchor), stay(frag_momentum))


def finish(
    gradient, weight, first, second, local, anchor, momentum,
    weight_out, first_out, second_out, local_out, anchor_out, momentum_out,
):
    slope = gradient[...]
    moment_one = beta_one * first[0].astype(jnp.float32) + (1.0 - beta_one) * slope
    moment_two = beta_two * second[0].astype(jnp.float32) + (1.0 - beta_two) * slope * slope
    step_size = moment_one / bias_one / (jnp.sqrt(moment_two / bias_two) + epsilon)
    master = weight[0]
    weight_out[0] = master - inner_rate * (step_size + weight_decay * master)
    first_out[0] = moment_one.astype(jnp.bfloat16)
    second_out[0] = moment_two.astype(jnp.bfloat16)
    local_out[0] = local[...]
    anchor_out[...] = anchor[...]
    momentum_out[...] = momentum[...]


def finished(gradient, weight, first, second, local, anchor, momentum):
    vmem = pl.BlockSpec(memory_space=pltpu.VMEM)
    shape = jax.ShapeDtypeStruct
    return pl.pallas_call(
        finish,
        out_shape=(
            shape(weight.shape, weight.dtype),
            shape(first.shape, first.dtype),
            shape(second.shape, second.dtype),
            shape(weight.shape, local.dtype),
            shape(anchor.shape, anchor.dtype),
            shape(momentum.shape, momentum.dtype),
        ),
        in_specs=[vmem] * 7,
        out_specs=(vmem,) * 6,
        compiler_params=pltpu.CompilerParams(vmem_limit_bytes=16 * 1024 * 1024),
        name="finish",
    )(gradient, weight, first, second, local, anchor, momentum)


def per_device(
    hidden,
    cotangent,
    weight,
    first_moment,
    second_moment,
    sync_frag,
    frag_local,
    frag_anchor,
    frag_momentum,
):
    gradient, new_local, anchor_out, momentum_out = reduced(
        hidden, cotangent, sync_frag, frag_local, frag_anchor, frag_momentum
    )
    return finished(
        gradient, weight, first_moment, second_moment, new_local, anchor_out, momentum_out
    )


def solution(mesh):
    in_specs = (
        P("group", "fsdp", None),
        P("group", "fsdp", None),
        P("group", "fsdp", None),
        P("group", "fsdp", None),
        P("group", "fsdp", None),
        P(),
        P("group", "fsdp", None),
        P(None, ("fsdp", "group"), None),
        P(None, ("fsdp", "group"), None),
    )
    out_specs = (
        P("group", "fsdp", None),
        P("group", "fsdp", None),
        P("group", "fsdp", None),
        P("group", "fsdp", None),
        P(("fsdp", "group"), None),
        P(("fsdp", "group"), None),
    )
    return jax.shard_map(
        per_device, mesh=mesh, in_specs=in_specs, out_specs=out_specs, check_vma=False
    )
```
